256 devices in a mesh: dp: 4 (over x), ctx: 8 (over y, core), tp: 8 (over z).
Axes of the slice: x: 4, y: 4, z: 8, core: 2. Of those that a mesh axis runs over, the one named last changes fastest.
Arguments:
- hidden: bfloat16 [4, 2048, 8192], P('dp', ('ctx', 'tp')), may hold values from -6 to 6
- key_weight: bfloat16 [8192, 1024], P(None, 'tp'), may hold values from -0.0625 to 0.0625
- value_weight: bfloat16 [8192, 1024], P(None, 'tp'), may hold values from -0.0625 to 0.0625
- queries: bfloat16 [4, 2048, 8192], P('dp', 'ctx', 'tp'), may hold values from -200 to 200
- out_grad: bfloat16 [4, 2048, 8192], P('dp', 'ctx', 'tp'), may hold values from -6 to 6
- segment_ids: int32 [4, 2048], P('dp', 'ctx'), may hold values from 0 to 7, never falling along the last dimension, each value on 1 to 1024 neighbouring positions
Outputs:
- attended: bfloat16 [4, 2048, 8192], P('dp', 'ctx', 'tp')
- query_grad: bfloat16 [4, 2048, 8192], P('dp', 'ctx', 'tp')
- hidden_grad: bfloat16 [4, 2048, 8192], P('dp', ('ctx', 'tp'))
- key_weight_grad: float32 [8192, 1024], P(('dp', 'ctx'), 'tp')
- value_weight_grad: float32 [8192, 1024], P(('dp', 'ctx'), 'tp')
The draws below stay inside these ranges and needn't reach their ends.
Inputs may be any that keep to these rules, and one draw needn't show every extreme that they name: `segment_ids`: document numbers never fall along a bin, each document holds 1 to 1024 tokens, and one holds exactly 1024.
All inputs are finite; a program needn't handle non-finite values.
Results may differ from the reference program's by a relative error of at most 0.03.
The reference program's roundings to bfloat16 on the way (of `prob_b` and `dscore_b`) count: a program that leaves them out, or rounds other values in their place, can miss the bound.
Values may be sent and summed in bfloat16 or wider, within the bound.
No kernel may reach another device: no remote copies, remote signals or barrier semaphores. Data moves between devices by JAX's collectives and lax.ppermute only.
A program may use at most 128 MiB of HBM per device.

```python
import math
import jax
import jax.numpy as jnp
import numpy as np
from jax import lax

D = 8192
HQ = 64
KVH = 8
HD = 128
LEN = 2048
DOCS = 8
BINS = 4


def draw_queries(key, part):
    key = jax.random.fold_in(key, 7)
    base = jax.random.truncated_normal(key, -6.0, 6.0, (BINS, LEN, HQ * HD), jnp.float32)
    return base.astype(jnp.bfloat16)


def block_scale(own_key, dims, cuts, least, high):
    gain, own = 1.0, jax.random.fold_in(own_key, 6)
    for dim, shards_of in cuts:
        heights = jnp.exp(jax.random.uniform(jax.random.fold_in(own, dim), (shards_of,), jnp.float32, least / len(cuts), high / len(cuts)))
        gain = gain * jnp.repeat(heights, dims[dim] // shards_of).reshape([-1 if axis == dim else 1 for axis in range(len(dims))])
    return gain


def split_up(count, total, bound, slope):
    weights = [(1 << 20) // math.isqrt(grade ** slope) + 1 for grade in range(2, count + 1)]
    spare, holding = total - bound - (count - 1), [1] * (count - 1)
    while spare > 0:
        movable = [i for i in range(count - 1) if holding[i] < bound]
        whole, budget = sum([weights[i] for i in movable]), spare
        for i in movable:
            addition = min(bound - holding[i], max(1, budget * weights[i] // whole), spare)
            holding[i] = holding[i] + addition
            spare = spare - addition
    return np.array([bound] + holding)


def uneven(stream_key, amount, total, reach, skew):
    if amount == 2:
        one = jax.random.randint(stream_key, (), max(1, total - reach), min(reach, total - 1) + 1)
        return jnp.stack([one, total - one])
    lengths = jnp.asarray(split_up(amount, total, reach, skew), jnp.int32)
    twos = (amount - 1) // 2
    donor, taker = lengths[1:1 + 2 * twos:2], lengths[2:2 + 2 * twos:2]
    room = jnp.minimum(donor - 1, reach - taker)
    shifted = jax.random.randint(jax.random.fold_in(stream_key, 1), (twos,), 0, 1 << 20) % (room + 1)
    lengths = lengths.at[1:1 + 2 * twos:2].set(donor - shifted).at[2:2 + 2 * twos:2].set(taker + shifted)
    return lengths[jax.random.permutation(jax.random.fold_in(stream_key, 2), amount)]


def centred(rng, dims, scale, reach, pieces=(), dtype=jnp.bfloat16):
    drawn = scale * jax.random.normal(rng, dims, jnp.float32)
    if pieces:
        drawn = drawn * block_scale(rng, dims, pieces, -0.22, 0.18)
    return jnp.clip(drawn, -reach, reach).astype(dtype)


def setup_inputs(seed: int = 0) -> dict:
    key_list = jax.random.split(jax.random.key(seed), 7)
    hidden = centred(key_list[0], (BINS, LEN, D), 1.0, 6.0, ((0, 4), (1, 64)))
    key_weight = centred(key_list[1], (D, KVH * HD), D ** -0.5, 0.0625, ((1, 8),))
    value_weight = centred(key_list[2], (D, KVH * HD), D ** -0.5, 0.0625, ((1, 8),))
    queries = draw_queries(jax.random.fold_in(key_list[6], 71), 0)
    out_grad = centred(key_list[4], (BINS, LEN, HQ * HD), 1.0, 6.0, ((0, 4), (1, 8), (2, 8)))
    segment_ids = jax.vmap(lambda own: jnp.searchsorted(jnp.cumsum(uneven(own, DOCS, LEN, LEN // 2, 1)), jnp.arange(LEN), side="right"))(jax.random.split(key_list[5], BINS)).reshape((BINS, LEN)).astype(jnp.int32)
    return dict(hidden=hidden, key_weight=key_weight, value_weight=value_weight, queries=queries, out_grad=out_grad, segment_ids=segment_ids)


def head_pass(args, mask):
    qh, kh, vh, doh = args
    scale = 1.0 / math.sqrt(HD)
    q32 = qh.astype(jnp.float32)
    k32 = kh.astype(jnp.float32)
    v32 = vh.astype(jnp.float32)
    do32 = doh.astype(jnp.float32)
    scores = jnp.einsum('qgd,kd->gqk', q32, k32) * scale
    scores = jnp.where(mask[None], scores, -jnp.inf)
    top = lax.optimization_barrier(jnp.max(scores, axis=-1, keepdims=True))
    expd = jnp.exp(scores - top)
    prob = expd / lax.optimization_barrier(jnp.sum(expd, axis=-1, keepdims=True))
    prob_b = lax.optimization_barrier(prob.astype(jnp.bfloat16)).astype(jnp.float32)
    attended = jnp.einsum('gqk,kd->qgd', prob_b, v32).astype(jnp.bfloat16)
    delta = jnp.transpose(lax.optimization_barrier(jnp.sum(do32 * attended.astype(jnp.float32), axis=-1)))
    dprob = jnp.einsum('qgd,kd->gqk', do32, v32)
    dscore = prob * (dprob - delta[:, :, None])
    dscore_b = lax.optimization_barrier(dscore.astype(jnp.bfloat16)).astype(jnp.float32)
    query_grad = (jnp.einsum('gqk,kd->qgd', dscore_b, k32) * scale).astype(jnp.bfloat16)
    key_grad = jnp.einsum('gqk,qgd->kd', dscore_b, q32) * scale
    value_grad = jnp.einsum('gqk,qgd->kd', prob_b, do32)
    return (attended, query_grad, key_grad, value_grad)

def reference(hidden, key_weight, value_weight, queries, out_grad, segment_ids):
    group = HQ // KVH
    places = jnp.arange(LEN).astype(jnp.int32)
    outs_att, outs_dq, outs_dx = ([], [], [])
    key_wgrad = jnp.zeros((D, KVH * HD), jnp.float32)
    value_wgrad = jnp.zeros((D, KVH * HD), jnp.float32)
    for index in range(BINS):
        inputs = hidden[index]
        keys = jnp.dot(inputs, key_weight, preferred_element_type=jnp.float32).astype(jnp.bfloat16)
        values = jnp.dot(inputs, value_weight, preferred_element_type=jnp.float32).astype(jnp.bfloat16)
        seg = segment_ids[index]
        mask = (seg[:, None] == seg[None, :]) & (places[None, :] <= places[:, None])
        qh = jnp.transpose(queries[index].reshape(LEN, KVH, group, HD), (1, 0, 2, 3))
        doh = jnp.transpose(out_grad[index].reshape(LEN, KVH, group, HD), (1, 0, 2, 3))
        kh = jnp.transpose(keys.reshape(LEN, KVH, HD), (1, 0, 2))
        vh = jnp.transpose(values.reshape(LEN, KVH, HD), (1, 0, 2))
        att, dq, dk, dv = lax.map(lambda a: head_pass(a, mask), (qh, kh, vh, doh))
        outs_att.append(jnp.transpose(att, (1, 0, 2, 3)).reshape(LEN, HQ * HD))
        outs_dq.append(jnp.transpose(dq, (1, 0, 2, 3)).reshape(LEN, HQ * HD))
        dk_b = jnp.transpose(dk, (1, 0, 2)).reshape(LEN, KVH * HD).astype(jnp.bfloat16)
        dv_b = jnp.transpose(dv, (1, 0, 2)).reshape(LEN, KVH * HD).astype(jnp.bfloat16)
        dx = jnp.dot(dk_b, key_weight.T, preferred_element_type=jnp.float32) + jnp.dot(dv_b, value_weight.T, preferred_element_type=jnp.float32)
        outs_dx.append(dx.astype(jnp.bfloat16))
        key_wgrad = key_wgrad + jnp.dot(inputs.T, dk_b, preferred_element_type=jnp.float32)
        value_wgrad = value_wgrad + jnp.dot(inputs.T, dv_b, preferred_element_type=jnp.float32)
    return (jnp.stack(outs_att), jnp.stack(outs_dq), jnp.stack(outs_dx), key_wgrad, value_wgrad)
```

```python
import functools
import math

import jax
import jax.numpy as jnp
from jax import lax
from jax.experimental import pallas as pl
from jax.experimental.pallas import tpu as pltpu
from jax.sharding import Mesh, PartitionSpec as P

HD = 128
SLOTS = 5
NEG = -1e30
F32 = jnp.float32
BF16 = jnp.bfloat16


def attention_kernel(thr_ref, kv0, kv1, kv2, kv3, kv4, q_ref, do_ref,
                     att_ref, dq_ref, dkv_ref, k_all, v_all, kt_all, vt_all, s_ref, pb_ref):
    rows = q_ref.shape[0]
    scale = 1.0 / math.sqrt(HD)
    log2e = math.log2(math.e)
    head = pl.program_id(0)

    @pl.when(head == 0)
    def _():
        for j, kv in enumerate((kv0, kv1, kv2, kv3, kv4)):
            here = pl.ds(j * rows, rows)
            k = kv[:, :HD]
            v = kv[:, HD:]
            k_all[here, :] = k
            v_all[here, :] = v
            kt_all[:, here] = k.T
            vt_all[:, here] = v.T
        dkv_ref[...] = jnp.zeros_like(dkv_ref)

    q = q_ref[...]
    do = do_ref[...]
    top = jnp.full((1, rows), NEG, F32)
    place = lax.broadcasted_iota(jnp.int32, (rows, rows), 0)
    for j in range(SLOTS):
        here = pl.ds(j * rows, rows)
        s = lax.dot_general(k_all[here, :], q, (((1,), (1,)), ((), ())), preferred_element_type=F32)
        mask = place >= thr_ref[j:j + 1, :]
        if j == 0:
            mask = mask & (place <= lax.broadcasted_iota(jnp.int32, (rows, rows), 1))
        s = jnp.where(mask, s, NEG)
        s_ref[here, :] = s
        top = jnp.maximum(top, jnp.max(s, axis=0, keepdims=True))
    total = jnp.zeros((1, rows), F32)
    for j in range(SLOTS):
        here = pl.ds(j * rows, rows)
        e = jnp.exp2((s_ref[here, :] - top) * (scale * log2e))
        s_ref[here, :] = e
        total = total + jnp.sum(e, axis=0, keepdims=True)
    inv = 1.0 / total
    out_t = jnp.zeros((HD, rows), F32)
    for j in range(SLOTS):
        here = pl.ds(j * rows, rows)
        prob = s_ref[here, :] * inv
        s_ref[here, :] = prob
        prob_b = prob.astype(BF16)
        pb_ref[here, :] = prob_b
        out_t = out_t + jnp.dot(vt_all[:, here], prob_b, preferred_element_type=F32)
    out_b = out_t.astype(BF16)
    att_ref[...] = out_b.T
    delta = jnp.sum(do.T.astype(F32) * out_b.astype(F32), axis=0, keepdims=True)
    dq_t = jnp.zeros((HD, rows), F32)
    for j in range(SLOTS):
        here = pl.ds(j * rows, rows)
        dp = lax.dot_general(v_all[here, :], do, (((1,), (1,)), ((), ())), preferred_element_type=F32)
        ds = (s_ref[here, :] * (dp - delta)).astype(BF16)
        dq_t = dq_t + jnp.dot(kt_all[:, here], ds, preferred_element_type=F32)
        dkv_ref[here, :HD] += jnp.dot(ds, q, preferred_element_type=F32)
        dkv_ref[here, HD:] += jnp.dot(pb_ref[here, :], do, preferred_element_type=F32)
    dq_ref[...] = (dq_t * scale).astype(BF16).T

    @pl.when(head == pl.num_programs(0) - 1)
    def _():
        dkv_ref[:, :HD] = dkv_ref[:, :HD] * scale


def attention(thr, slots, q, do):
    rows, width = q.shape
    heads = width // HD
    whole = lambda h: (0, 0)
    return pl.pallas_call(
        attention_kernel,
        grid=(heads,),
        in_specs=[pl.BlockSpec(thr.shape, whole)]
        + [pl.BlockSpec((rows, 2 * HD), whole)] * SLOTS
        + [pl.BlockSpec((rows, HD), lambda h: (0, h))] * 2,
        out_specs=[
            pl.BlockSpec((rows, HD), lambda h: (0, h)),
            pl.BlockSpec((rows, HD), lambda h: (0, h)),
            pl.BlockSpec((SLOTS * rows, 2 * HD), whole),
        ],
        out_shape=[
            jax.ShapeDtypeStruct((rows, width), BF16),
            jax.ShapeDtypeStruct((rows, width), BF16),
            jax.ShapeDtypeStruct((SLOTS * rows, 2 * HD), F32),
        ],
        scratch_shapes=[
            pltpu.VMEM((SLOTS * rows, HD), BF16),
            pltpu.VMEM((SLOTS * rows, HD), BF16),
            pltpu.VMEM((HD, SLOTS * rows), BF16),
            pltpu.VMEM((HD, SLOTS * rows), BF16),
            pltpu.VMEM((SLOTS * rows, rows), F32),
            pltpu.VMEM((SLOTS * rows, rows), BF16),
        ],
        compiler_params=pltpu.CompilerParams(
            dimension_semantics=("arbitrary",), vmem_limit_bytes=40 * 1024 * 1024
        ),
        cost_estimate=pl.CostEstimate(
            flops=12 * SLOTS * rows * width * rows, bytes_accessed=6 * 1024 * 1024,
            transcendentals=SLOTS * rows * rows * heads,
        ),
    )(thr, *slots, q, do)


def on_device(hidden, key_weight, value_weight, queries, out_grad, segment_ids):
    rows = queries.shape[1]
    width = hidden.shape[2]
    x_count = hidden.shape[1]
    ny = lax.axis_size("y")
    chips = lax.axis_size("dp") * ny
    y = lax.axis_index("y")
    core = lax.axis_index("core")
    swap = [(0, 1), (1, 0)]

    gathered = lax.all_gather(hidden[0], "tp", axis=0, tiled=True)
    weights = jnp.concatenate([key_weight, value_weight], axis=1)

    all_seg = lax.all_gather(segment_ids[0], ("y", "core"), axis=0, tiled=True)
    starts = jnp.sum(
        (all_seg[None, :] < segment_ids[0][:, None]).astype(jnp.int32), axis=1
    ) - (2 * y + core) * rows
    back3 = jnp.where(core == 0, 1, 3) * rows
    back4 = jnp.where(core == 0, 3, 1) * rows
    backs = jnp.stack([jnp.int32(0), jnp.int32(2 * rows), jnp.int32(4 * rows), back3, back4])
    thr = starts[None, :] + jnp.concatenate([backs, jnp.zeros((3,), jnp.int32)])[:, None]

    kv = jnp.dot(gathered, weights, preferred_element_type=F32).astype(BF16)

    down1 = [(i, i + 1) for i in range(ny - 1)]
    down2 = [(i, i + 2) for i in range(ny - 2)]
    kv1 = lax.ppermute(kv, "y", down1)
    kv2 = lax.ppermute(kv, "y", down2)
    near = lax.ppermute(kv, "core", [(0, 1)])
    kv3 = lax.ppermute(kv1, "core", swap)
    far = lax.ppermute(kv2, "core", [(1, 0)])
    kv4 = jnp.where(core == 0, far, near)

    att, dq, dkv = attention(thr, (kv, kv1, kv2, kv3, kv4), queries[0], out_grad[0])

    cols = gathered.reshape(rows, chips, 2, width // (2 * chips))
    mine = jnp.where(core == 0, cols[:, :, 0], cols[:, :, 1])
    theirs = jnp.where(core == 0, cols[:, :, 1], cols[:, :, 0])
    other = lax.ppermute(theirs, "core", swap)

    part = dkv.reshape(SLOTS, rows, 2 * HD)
    up1 = [(i + 1, i) for i in range(ny - 1)]
    up2 = [(i + 2, i) for i in range(ny - 2)]
    got3 = lax.ppermute(part[3], "core", swap)
    got4 = lax.ppermute(part[4], "core", swap)
    own = part[0] + jnp.where(core == 0, got4, 0.0)
    send1 = (part[1] + got3).astype(BF16)
    send2 = (part[2] + jnp.where(core == 0, 0.0, got4)).astype(BF16)
    got1 = lax.ppermute(send1, "y", up1)
    got2 = lax.ppermute(send2, "y", up2)
    grads = (own + got1.astype(F32) + got2.astype(F32)).astype(BF16)

    spread = lax.dot_general(
        grads, weights, (((1,), (1,)), ((), ())), preferred_element_type=F32
    ).astype(BF16)
    hidden_grad = lax.psum_scatter(spread, "tp", scatter_dimension=0, tiled=True)

    other_grads = lax.ppermute(grads, "core", swap)
    contract = (((0,), (0,)), ((), ()))
    half = lax.dot_general(
        grads, mine.reshape(rows, -1), contract, preferred_element_type=F32
    ) + lax.dot_general(
        other_grads, other.reshape(rows, -1), contract, preferred_element_type=F32
    )
    blocks = jnp.transpose(half.astype(BF16).reshape(2 * HD, chips, -1), (1, 0, 2))
    blocks = lax.all_to_all(blocks, ("dp", "y"), 0, 0, tiled=True)
    summed = jnp.sum(blocks.astype(F32), axis=0).T
    return (
        att[None],
        dq[None],
        hidden_grad.reshape(1, x_count, width),
        summed[:, :HD],
        summed[:, HD:],
    )


def solution(mesh):
    fine = Mesh(
        mesh.devices.reshape(mesh.shape["dp"], mesh.shape["ctx"] // 2, 2, mesh.shape["tp"]),
        ("dp", "y", "core", "tp"),
    )
    ctx = ("y", "core")
    in_specs = (
        P("dp", ("y", "core", "tp"), None),
        P(None, "tp"),
        P(None, "tp"),
        P("dp", ctx, "tp"),
        P("dp", ctx, "tp"),
        P("dp", ctx),
    )
    out_specs = (
        P("dp", ctx, "tp"),
        P("dp", ctx, "tp"),
        P("dp", ("y", "core", "tp"), None),
        P(("dp", "y", "core"), "tp"),
        P(("dp", "y", "core"), "tp"),
    )
    return jax.shard_map(
        on_device, mesh=fine, in_specs=in_specs, out_specs=out_specs, check_vma=False
    )
```

```python
import functools
import math

import jax
import jax.numpy as jnp
from jax import lax
from jax.experimental import pallas as pl
from jax.experimental.pallas import tpu as pltpu
from jax.sharding import Mesh, PartitionSpec as P

HD = 128
SLOTS = 5
PAIR = 2
EARLY = [(s, h) for s in (0, 1, 7, 2, 6) for h in (0, 1)] + [(3, 0), (5, 1)]
LATE = [(3, 1), (5, 0), (4, 0), (4, 1)]
NEG = -1e30
MIB = 1024 * 1024
VMEM = 56 * MIB
F32 = jnp.float32
BF16 = jnp.bfloat16


def attention_kernel(place_ref, kv0, kv1, kv2, kv3, near, far, q_ref, do_ref,
                     att_ref, dq_ref, p0, p1, p2, p34,
                     k_all, v_all, kt_all, vt_all, s_ref, pb_ref, ds_ref, dkv_ref, thr_ref):
    rows = q_ref.shape[0]
    scale = 1.0 / math.sqrt(HD)
    log2e = math.log2(math.e)
    step = pl.program_id(0)
    heads = range(PAIR)
    spans = [pl.ds(j * rows, rows) for j in range(SLOTS)]

    @pl.when(step == 0)
    def _():
        blocks = (kv0[...], kv1[...], kv2[...], kv3[...], near[...] + far[...])
        documents = [kv[rows:, :].astype(F32) for kv in blocks]
        start = jnp.full((1, rows), (1 - SLOTS) * rows, jnp.int32)
        for doc in documents:
            earlier = doc.T[:, :1] < documents[0][:1, :]
            start = start + jnp.sum(earlier.astype(jnp.int32), axis=0, keepdims=True)
        core = place_ref[2]
        for j, back in enumerate((0, 2, 4, 1 + 2 * core, 3 - 2 * core)):
            thr_ref[j:j + 1, :] = start + back * rows
        for here, kv in zip(spans, blocks):
            k = kv[:rows, :HD]
            v = kv[:rows, HD:]
            k_all[here, :] = k
            v_all[here, :] = v
            kt_all[:, here] = k.T
            vt_all[:, here] = v.T
        dkv_ref[...] = jnp.zeros_like(dkv_ref)

    q = [q_ref[:, h * HD:(h + 1) * HD] for h in heads]
    do = [do_ref[:, h * HD:(h + 1) * HD] for h in heads]
    q_t = [a.T for a in q]
    do_t = [a.T for a in do]
    top = [jnp.full((1, rows), NEG, F32) for _ in heads]
    place = lax.broadcasted_iota(jnp.int32, (rows, rows), 0)
    for j, here in enumerate(spans):
        mask = place >= thr_ref[j:j + 1, :]
        if j == 0:
            mask = mask & (place <= lax.broadcasted_iota(jnp.int32, (rows, rows), 1))
        for h in heads:
            s = jnp.dot(k_all[here, :], q_t[h], preferred_element_type=F32)
            s = jnp.where(mask, s, NEG)
            s_ref[h, here, :] = s
            top[h] = jnp.maximum(top[h], jnp.max(s, axis=0, keepdims=True))
    total = [jnp.zeros((1, rows), F32) for _ in heads]
    for here in spans:
        for h in heads:
            e = jnp.exp2((s_ref[h, here, :] - top[h]) * (scale * log2e))
            s_ref[h, here, :] = e
            total[h] = total[h] + jnp.sum(e, axis=0, keepdims=True)
    inv = [1.0 / t for t in total]
    for here in spans:
        for h in heads:
            pb_ref[h, here, :] = (s_ref[h, here, :] * inv[h]).astype(BF16)
    delta = []
    for h in heads:
        out_b = jnp.dot(vt_all[...], pb_ref[h], preferred_element_type=F32).astype(BF16)
        att_ref[:, h * HD:(h + 1) * HD] = out_b.T
        delta.append(jnp.sum(do_t[h].astype(F32) * out_b.astype(F32), axis=0, keepdims=True))
    for here in spans:
        dk = jnp.zeros((rows, HD), F32)
        dv = jnp.zeros((rows, HD), F32)
        for h in heads:
            dp = jnp.dot(v_all[here, :], do_t[h], preferred_element_type=F32)
            ds = (s_ref[h, here, :] * inv[h] * (dp - delta[h])).astype(BF16)
            ds_ref[h, here, :] = ds
            dk = dk + jnp.dot(ds, q[h], preferred_element_type=F32)
            dv = dv + jnp.dot(pb_ref[h, here, :], do[h], preferred_element_type=F32)
        dkv_ref[here, :HD] += dk
        dkv_ref[here, HD:] += dv
    for h in heads:
        dq_t = jnp.dot(kt_all[...], ds_ref[h], preferred_element_type=F32)
        dq_ref[:, h * HD:(h + 1) * HD] = (dq_t * scale).astype(BF16).T

    @pl.when(step == pl.num_programs(0) - 1)
    def _():
        for here, out in zip(spans, (p0, p1, p2, p34.at[0], p34.at[1])):
            out[:, :HD] = dkv_ref[here, :HD] * scale
            out[:, HD:] = dkv_ref[here, HD:]


def attention(place, slots, q, do):
    rows, width = q.shape
    heads = width // HD
    keys = SLOTS * rows
    whole = lambda h, place: (0, 0)
    square = pl.BlockSpec((rows, 2 * HD), whole)
    pair = pl.BlockSpec((rows, PAIR * HD), lambda h, place: (0, h))
    part = jax.ShapeDtypeStruct((rows, 2 * HD), F32)
    return pl.pallas_call(
        attention_kernel,
        grid_spec=pltpu.PrefetchScalarGridSpec(
            num_scalar_prefetch=1,
            grid=(heads // PAIR,),
            in_specs=[pl.BlockSpec(slots[0].shape, whole)] * len(slots) + [pair] * 2,
            out_specs=[
                pair, pair, square, square, square,
                pl.BlockSpec((2, rows, 2 * HD), lambda h, place: (0, 0, 0)),
            ],
            scratch_shapes=[
                pltpu.VMEM((keys, HD), BF16),
                pltpu.VMEM((keys, HD), BF16),
                pltpu.VMEM((HD, keys), BF16),
                pltpu.VMEM((HD, keys), BF16),
                pltpu.VMEM((PAIR, keys, rows), F32),
                pltpu.VMEM((PAIR, keys, rows), BF16),
                pltpu.VMEM((PAIR, keys, rows), BF16),
                pltpu.VMEM((keys, 2 * HD), F32),
                pltpu.VMEM((8, rows), jnp.int32),
            ],
        ),
        out_shape=[
            jax.ShapeDtypeStruct((rows, width), BF16),
            jax.ShapeDtypeStruct((rows, width), BF16),
            part, part, part,
            jax.ShapeDtypeStruct((2, rows, 2 * HD), F32),
        ],
        compiler_params=pltpu.CompilerParams(vmem_limit_bytes=20 * MIB),
        cost_estimate=pl.CostEstimate(
            flops=12 * keys * width * rows, bytes_accessed=6 * MIB,
            transcendentals=keys * rows * heads,
        ),
    )(place, *slots, q, do)


def token(place, s, h, ring, few):
    return pl.multiple_of((lax.rem(place[3] + ring - s, ring) * 2 + h) * few, few)


def project_kernel(order, ring, last, place_ref, *refs):
    pieces, refs = refs[:len(order)], refs[len(order):]
    if last:
        wk_hbm, wv_hbm, seg_ref, early_ref, refs = *refs[:4], refs[6:]
    else:
        wk_hbm, wv_hbm, refs = *refs[:2], refs[2:]
    kv_ref, mine_hbm, theirs_hbm, h_ref, w_ref, come, come_w, go = refs
    few = pieces[0].shape[0]
    rows, width = h_ref.shape
    block = 2 * HD
    steps = come_w.shape[0] // 2
    depth = width // steps

    copies = [
        pltpu.make_async_copy(piece, h_ref.at[pl.ds(i * few, few), :], come.at[i])
        for i, piece in enumerate(pieces)
    ]
    weights = []
    for c in range(steps):
        at = pl.ds(c * depth, depth)
        weights.append([
            pltpu.make_async_copy(
                w.at[at, :], w_ref.at[at, pl.ds(i * HD, HD)], come_w.at[2 * c + i]
            )
            for i, w in enumerate((wk_hbm, wv_hbm))
        ])
    for copy in weights[0] + copies + sum(weights[1:], []):
        copy.start()
    for copy in copies:
        copy.wait()
    out = []
    base = 0 if not last else len(EARLY) * few
    for i in range(width // block):
        core, to = ((1 - place_ref[2], theirs_hbm), (place_ref[2], mine_hbm))[i % 2]
        first = pl.multiple_of((2 * (i // 2) + core) * block, block)
        out.append(pltpu.make_async_copy(
            h_ref.at[:, pl.ds(first, block)],
            to.at[pl.ds(base, rows), pl.ds(i // 2 * block, block)],
            go.at[i],
        ))
        out[-1].start()
    kv = jnp.zeros((rows, 2 * HD), F32)
    for c in range(steps):
        for copy in weights[c]:
            copy.wait()
        at = slice(c * depth, (c + 1) * depth)
        kv = kv + jnp.dot(h_ref[:, at], w_ref[at, :], preferred_element_type=F32)
    kv = kv.astype(BF16)
    if not last:
        kv_ref[...] = kv
    else:
        for i, (s, h) in enumerate(order):
            kv_ref[pl.ds(token(place_ref, s, h, ring, few), few), :] = kv[i * few:(i + 1) * few]
        for i, (s, h) in enumerate(EARLY):
            to = pl.ds(token(place_ref, s, h, ring, few), few)
            kv_ref[to, :] = early_ref[i * few:(i + 1) * few, :]
        total = seg_ref.shape[1]
        own = (seg_ref[...] + 1).astype(F32)
        kv_ref[total:, :] = jnp.broadcast_to(own, (kv_ref.shape[0] - total, total)).astype(BF16)
    for copy in out:
        copy.wait()


def project(place, order, pieces, key_weight, value_weight, ring, rest=()):
    few, width = pieces[0].shape
    rows = few * len(pieces)
    total = few * 2 * ring
    steps = 4
    far = pl.BlockSpec(memory_space=pl.ANY)
    whole = lambda i, place: (0, 0)
    kv_rows = total + 16 if rest else rows
    n = len(pieces)
    return pl.pallas_call(
        functools.partial(project_kernel, order, ring, bool(rest)),
        grid_spec=pltpu.PrefetchScalarGridSpec(
            num_scalar_prefetch=1,
            grid=(1,),
            in_specs=[far] * (n + 2)
            + ([pl.BlockSpec(a.shape, whole) for a in rest[:2]] + [far, far] if rest else []),
            out_specs=[pl.BlockSpec((kv_rows, 2 * HD), whole), far, far],
            scratch_shapes=[
                pltpu.VMEM((rows, width), BF16),
                pltpu.VMEM((width, 2 * HD), BF16),
                pltpu.SemaphoreType.DMA((n,)),
                pltpu.SemaphoreType.DMA((2 * steps,)),
                pltpu.SemaphoreType.DMA((width // (2 * HD),)),
            ],
        ),
        out_shape=[
            jax.ShapeDtypeStruct((kv_rows, 2 * HD), BF16),
            jax.ShapeDtypeStruct((total, width // 2), BF16),
            jax.ShapeDtypeStruct((total, width // 2), BF16),
        ],
        input_output_aliases={n + 5: 1, n + 6: 2} if rest else {},
        compiler_params=pltpu.CompilerParams(vmem_limit_bytes=VMEM),
        cost_estimate=pl.CostEstimate(
            flops=4 * rows * width * HD, bytes_accessed=8 * MIB, transcendentals=0
        ),
    )(place, *pieces, key_weight, value_weight, *rest)


def weight_grad_kernel(ring, place_ref, g_ref, gs_ref, *refs):
    hidden, (out_ref, grads_t, turn) = refs[:8], refs[8:]
    nx = out_ref.shape[1]
    few = g_ref.shape[0] // (2 * ring)

    @pl.when(pl.program_id(0) == 0)
    def _():
        for p, g in enumerate((g_ref, gs_ref)):
            for i, (s, h) in enumerate(EARLY + LATE):
                turn[i * few:(i + 1) * few, :] = g[pl.ds(token(place_ref, s, h, ring, few), few), :]
            grads_t[p] = turn[...].T

    for i, (mine, other) in enumerate(zip(hidden[:nx], hidden[nx:])):
        out_ref[0, lax.rem(i + nx - place_ref[0], nx)] = (
            jnp.dot(grads_t[0], mine[...], preferred_element_type=F32)
            + jnp.dot(grads_t[1], other[...], preferred_element_type=F32)
        ).astype(BF16)


def weight_grad(place, grads, other_grads, mine, other, nx, ny, ring):
    rows, cols = grads.shape
    block = mine.shape[1] // (nx * ny)
    flat = pl.BlockSpec((rows, cols), lambda r, place: (0, 0))

    def column(i):
        return pl.BlockSpec((rows, block), lambda r, place: (0, i * ny + r))

    return pl.pallas_call(
        functools.partial(weight_grad_kernel, ring),
        grid_spec=pltpu.PrefetchScalarGridSpec(
            num_scalar_prefetch=1,
            grid=(ny,),
            in_specs=[flat, flat] + [column(i) for i in range(nx)] * 2,
            out_specs=pl.BlockSpec((1, nx, cols, block), lambda r, place: (r, 0, 0, 0)),
            scratch_shapes=[pltpu.VMEM((2, cols, rows), BF16), pltpu.VMEM((rows, cols), BF16)],
        ),
        out_shape=jax.ShapeDtypeStruct((ny, nx, cols, block), BF16),
        compiler_params=pltpu.CompilerParams(vmem_limit_bytes=10 * MIB),
        cost_estimate=pl.CostEstimate(
            flops=4 * rows * cols * block * nx * ny, bytes_accessed=6 * MIB, transcendentals=0
        ),
    )(place, grads, other_grads, *[mine] * nx, *[other] * nx)


def add_kernel(parts, *outs):
    for i, out in enumerate(outs):
        total = parts[0, i].astype(F32)
        for r in range(1, parts.shape[0]):
            total = total + parts[r, i].astype(F32)
        out[...] = total.astype(BF16)


def add(parts):
    ny, nx, cols, block = parts.shape
    return pl.pallas_call(
        add_kernel,
        grid=(1,),
        in_specs=[pl.BlockSpec(parts.shape, lambda i: (0, 0, 0, 0))],
        out_specs=[pl.BlockSpec((cols, block), lambda i: (0, 0))] * nx,
        out_shape=[jax.ShapeDtypeStruct((cols, block), BF16)] * nx,
        compiler_params=pltpu.CompilerParams(vmem_limit_bytes=10 * MIB),
    )(parts)


def finish_kernel(a, b, c, d, key_ref, value_ref):
    total = (a[...].astype(F32) + b[...].astype(F32)) + (c[...].astype(F32) + d[...].astype(F32))
    key_ref[...] = total[:HD].T
    value_ref[...] = total[HD:].T


def finish(parts):
    cols, block = parts[0].shape
    half = pl.BlockSpec((block, HD), lambda i: (0, 0))
    shape = jax.ShapeDtypeStruct((block, HD), F32)
    return pl.pallas_call(
        finish_kernel,
        grid=(1,),
        in_specs=[pl.BlockSpec((cols, block), lambda i: (0, 0))] * 4,
        out_specs=[half, half],
        out_shape=[shape, shape],
        compiler_params=pltpu.CompilerParams(vmem_limit_bytes=8 * MIB),
    )(*parts)


def spread_kernel(b0, b1, b2, b3, wa_ref, wb_ref, o0, o1, o2, o3, left):
    few = o0.shape[1]
    heads = left.shape[0]

    @pl.when(pl.program_id(0) == 0)
    def _():
        for s, b in enumerate((b0, b1, b2, b3)):
            left[:, s * few:(s + 1) * few, :] = b[...]

    contract = (((1,), (1,)), ((), ()))
    for p, w in enumerate((wa_ref, wb_ref)):
        acc = lax.dot_general(w[0], left[0], contract, preferred_element_type=F32)
        for h in range(1, heads):
            acc = acc + lax.dot_general(w[h], left[h], contract, preferred_element_type=F32)
        turned = acc.T.astype(BF16)
        for s, out in enumerate((o0, o1, o2, o3)):
            out[p] = turned[s * few:(s + 1) * few]


def spread(blocks, wa, wb):
    heads, few, cols = blocks[0].shape
    depth = wa.shape[1]
    tile = depth // 4
    weight = pl.BlockSpec((heads, tile, cols), lambda i: (0, i, 0))
    return pl.pallas_call(
        spread_kernel,
        grid=(depth // tile,),
        in_specs=[pl.BlockSpec((heads, few, cols), lambda i: (0, 0, 0))] * 4 + [weight, weight],
        out_specs=[pl.BlockSpec((2, few, tile), lambda i: (0, 0, i))] * 4,
        out_shape=[jax.ShapeDtypeStruct((2, few, depth), BF16)] * 4,
        scratch_shapes=[pltpu.VMEM((heads, 4 * few, cols), BF16)],
        compiler_params=pltpu.CompilerParams(vmem_limit_bytes=VMEM),
        cost_estimate=pl.CostEstimate(
            flops=16 * few * heads * cols * depth, bytes_accessed=9 * MIB, transcendentals=0
        ),
    )(*blocks, wa, wb)


def assemble_kernel(place_ref, a, b, c, d, out_ref):
    depth = a.shape[2]
    for s, piece in enumerate((a, b, c, d)):
        part = lax.rem(place_ref[0] + s, 4) * 2
        for p in range(2):
            core = place_ref[2] if p == 0 else 1 - place_ref[2]
            out_ref[:, pl.ds(pl.multiple_of((part + core) * depth, depth), depth)] = piece[p]


def assemble(place, pieces):
    two, few, depth = pieces[0].shape
    return pl.pallas_call(
        assemble_kernel,
        grid_spec=pltpu.PrefetchScalarGridSpec(
            num_scalar_prefetch=1,
            grid=(1,),
            in_specs=[pl.BlockSpec((two, few, depth), lambda i, place: (0, 0, 0))] * 4,
            out_specs=pl.BlockSpec((few, 4 * two * depth), lambda i, place: (0, 0)),
        ),
        out_shape=jax.ShapeDtypeStruct((few, 4 * two * depth), BF16),
        compiler_params=pltpu.CompilerParams(vmem_limit_bytes=6 * MIB),
    )(place, *pieces)


def on_device(hidden, key_weight, value_weight, queries, out_grad, segment_ids):
    rows = queries.shape[1]
    x_count, width = hidden.shape[1:]
    nx = lax.axis_size("dp")
    ny = lax.axis_size("y")
    heads = lax.axis_size("tp")
    x = lax.axis_index("dp")
    core = lax.axis_index("core")
    place = jnp.stack([x, lax.axis_index("y"), core, lax.axis_index("tp")]).astype(jnp.int32)
    swap = [(0, 1), (1, 0)]

    def swapped(a):
        return lax.ppermute(a, "core", swap)

    def shifted(a, s, axis="dp"):
        n = lax.axis_size(axis)
        return lax.ppermute(a, axis, [(i, (i + s) % n) for i in range(n)])

    half = x_count // 2
    ring = {(0, h): hidden[0, h * half:(h + 1) * half] for h in range(2)}
    for s in range(1, heads // 2 + 1):
        for h in range(2):
            if s < heads // 2 or h == 0:
                ring[s, h] = shifted(ring[s - 1, h], 1, "tp")
            if s < heads // 2 or h == 1:
                ring[heads - s, h] = shifted(ring[(heads - s + 1) % heads, h], -1, "tp")
    weights = (key_weight, value_weight)
    early = project(place, EARLY, [ring[i] for i in EARLY], *weights, heads)
    kv, mine, theirs = project(
        place, LATE, [ring[i] for i in LATE], *weights, heads, (segment_ids, *early)
    )

    depth = width // (2 * nx)
    first = (x * 2 + core) * depth
    part_w = jnp.concatenate(
        [lax.dynamic_slice_in_dim(w, first, depth, axis=0) for w in (key_weight, value_weight)], axis=1
    )
    part_w, kv = lax.optimization_barrier((part_w, kv))
    all_w = lax.all_gather(part_w, "tp", axis=0)

    down1 = [(i, i + 1) for i in range(ny - 1)]
    down2 = [(i, i + 2) for i in range(ny - 2)]
    kv1 = lax.ppermute(kv, "y", down1)
    kv2 = lax.ppermute(kv, "y", down2)
    near = lax.ppermute(kv, "core", [(0, 1)])
    kv3 = swapped(kv1)
    far = lax.ppermute(kv2, "core", [(1, 0)])

    att, dq, part0, part1, part2, part34 = attention(
        place, (kv, kv1, kv2, kv3, near, far), queries[0], out_grad[0]
    )

    up1 = [(i + 1, i) for i in range(ny - 1)]
    up2 = [(i + 2, i) for i in range(ny - 2)]
    got = swapped(part34)
    send1 = (part1 + got[0]).astype(BF16)
    send2 = (part2 + jnp.where(core == 0, 0.0, got[1])).astype(BF16)
    own = part0 + jnp.where(core == 0, got[1], 0.0)
    got1 = lax.ppermute(send1, "y", up1)
    got2 = lax.ppermute(send2, "y", up2)
    grads = (own + got1.astype(F32) + got2.astype(F32)).astype(BF16)

    other = swapped(theirs)
    other_grads = swapped(grads)
    by_head = lax.all_to_all(grads.reshape(heads, x_count, 2 * HD), "tp", 0, 0, tiled=True)
    sums = weight_grad(place, grads, other_grads, mine, other, nx, ny, heads)
    by_head, sums, all_w = lax.optimization_barrier((by_head, sums, all_w))
    other_w = swapped(all_w)
    sums = lax.all_to_all(sums, "y", 0, 0, tiled=True)

    group_heads = [by_head] + [shifted(by_head, s) for s in range(1, nx)]
    pieces = spread(group_heads, all_w, other_w)
    _, sums = lax.optimization_barrier((pieces, sums))
    sums = add(sums)
    key_wgrad, value_wgrad = finish(
        [sums[0]] + [shifted(sums[s], s) for s in range(1, nx)]
    )
    hidden_grad = assemble(place, [pieces[0]] + [shifted(pieces[s], nx - s) for s in range(1, nx)])
    return (
        att[None],
        dq[None],
        hidden_grad[None],
        key_wgrad,
        value_wgrad,
    )


def solution(mesh):
    fine = Mesh(
        mesh.devices.reshape(mesh.shape["dp"], mesh.shape["ctx"] // 2, 2, mesh.shape["tp"]),
        ("dp", "y", "core", "tp"),
    )
    ctx = ("y", "core")
    in_specs = (
        P("dp", ("y", "core", "tp"), None),
        P(None, "tp"),
        P(None, "tp"),
        P("dp", ctx, "tp"),
        P("dp", ctx, "tp"),
        P("dp", ctx),
    )
    out_specs = (
        P("dp", ctx, "tp"),
        P("dp", ctx, "tp"),
        P("dp", ("y", "core", "tp"), None),
        P(("dp", "y", "core"), "tp"),
        P(("dp", "y", "core"), "tp"),
    )
    return jax.shard_map(
        on_device, mesh=fine, in_specs=in_specs, out_specs=out_specs, check_vma=False
    )
```

```python
import functools
import math

import jax
import jax.numpy as jnp
from jax import lax
from jax.experimental import pallas as pl
from jax.experimental.pallas import tpu as pltpu
from jax.sharding import Mesh, PartitionSpec as P

HD = 128
SLOTS = 5
PAIR = 4
EARLY = [(s, h) for s in (0, 1, 7, 2, 6) for h in (0, 1)] + [(3, 0), (5, 1)]
LATE = [(3, 1), (5, 0), (4, 0), (4, 1)]
FIRST = [(4, 0), (3, 1), (4, 1), (5, 0), (3, 0), (2, 1), (5, 1), (6, 0)]
REST = [(s, h) for s in range(8) for h in (0, 1) if (s, h) not in FIRST]
NEG = -1e30
MIB = 1024 * 1024
VMEM = 56 * MIB
F32 = jnp.float32
BF16 = jnp.bfloat16


def attention_kernel(place_ref, kv0, kv1, kv2, kv3, near, far, q_ref, do_ref,
                     att_ref, dq_ref, p0, p1, p2, p34,
                     k_all, v_all, kt_all, vt_all, s_ref, pb_ref, ds_ref, dp_ref, dkv_ref, thr_ref):
    rows = q_ref.shape[0]
    scale = 1.0 / math.sqrt(HD)
    log2e = math.log2(math.e)
    step = pl.program_id(0)
    heads = range(PAIR)
    spans = [pl.ds(j * rows, rows) for j in range(SLOTS)]

    @pl.when(step == 0)
    def _():
        blocks = (kv0[...], kv1[...], kv2[...], kv3[...], near[...] + far[...])
        documents = [kv[rows:, :].astype(F32) for kv in blocks]
        start = jnp.full((1, rows), (1 - SLOTS) * rows, jnp.int32)
        for doc in documents:
            earlier = doc.T[:, :1] < documents[0][:1, :]
            start = start + jnp.sum(earlier.astype(jnp.int32), axis=0, keepdims=True)
        core = place_ref[2]
        for j, back in enumerate((0, 2, 4, 1 + 2 * core, 3 - 2 * core)):
            thr_ref[j:j + 1, :] = start + back * rows
        for here, kv in zip(spans, blocks):
            k = kv[:rows, :HD]
            v = kv[:rows, HD:]
            k_all[here, :] = k
            v_all[here, :] = v
            kt_all[:, here] = k.T
            vt_all[:, here] = v.T
        dkv_ref[...] = jnp.zeros_like(dkv_ref)

    q = [q_ref[:, h * HD:(h + 1) * HD] for h in heads]
    do = [do_ref[:, h * HD:(h + 1) * HD] for h in heads]
    q_t = [a.T for a in q]
    do_t = [a.T for a in do]
    top = [jnp.full((1, rows), NEG, F32) for _ in heads]
    place = lax.broadcasted_iota(jnp.int32, (rows, rows), 0)
    for j, here in enumerate(spans):
        mask = place >= thr_ref[j:j + 1, :]
        if j == 0:
            mask = mask & (place <= lax.broadcasted_iota(jnp.int32, (rows, rows), 1))
        for h in heads:
            s = jnp.dot(k_all[here, :], q_t[h], preferred_element_type=F32)
            s = jnp.where(mask, s, NEG)
            s_ref[h, here, :] = s
            top[h] = jnp.maximum(top[h], jnp.max(s, axis=0, keepdims=True))
    total = [jnp.zeros((1, rows), F32) for _ in heads]
    for here in spans:
        for h in heads:
            e = jnp.exp2((s_ref[h, here, :] - top[h]) * (scale * log2e))
            s_ref[h, here, :] = e
            total[h] = total[h] + jnp.sum(e, axis=0, keepdims=True)
            dp_ref[h, here, :] = jnp.dot(v_all[here, :], do_t[h], preferred_element_type=F32)
    inv = [1.0 / t for t in total]
    for here in spans:
        for h in heads:
            pb_ref[h, here, :] = (s_ref[h, here, :] * inv[h]).astype(BF16)
    delta = []
    for h in heads:
        out_b = jnp.dot(vt_all[...], pb_ref[h], preferred_element_type=F32).astype(BF16)
        att_ref[:, h * HD:(h + 1) * HD] = out_b.T
        delta.append(jnp.sum(do_t[h].astype(F32) * out_b.astype(F32), axis=0, keepdims=True))
    for here in spans:
        dk = jnp.zeros((rows, HD), F32)
        dv = jnp.zeros((rows, HD), F32)
        for h in heads:
            ds = (s_ref[h, here, :] * inv[h] * (dp_ref[h, here, :] - delta[h])).astype(BF16)
            ds_ref[h, here, :] = ds
            dk = dk + jnp.dot(ds, q[h], preferred_element_type=F32)
            dv = dv + jnp.dot(pb_ref[h, here, :], do[h], preferred_element_type=F32)
        dkv_ref[here, :HD] += dk
        dkv_ref[here, HD:] += dv
    for h in heads:
        dq_t = jnp.dot(kt_all[...], ds_ref[h], preferred_element_type=F32)
        dq_ref[:, h * HD:(h + 1) * HD] = (dq_t * scale).astype(BF16).T

    @pl.when(step == pl.num_programs(0) - 1)
    def _():
        for here, out in zip(spans, (p0, p1, p2, p34.at[0], p34.at[1])):
            out[:, :HD] = dkv_ref[here, :HD] * scale
            out[:, HD:] = dkv_ref[here, HD:]


def attention(place, slots, q, do):
    rows, width = q.shape
    heads = width // HD
    keys = SLOTS * rows
    whole = lambda h, place: (0, 0)
    square = pl.BlockSpec((rows, 2 * HD), whole)
    pair = pl.BlockSpec((rows, PAIR * HD), lambda h, place: (0, h))
    part = jax.ShapeDtypeStruct((rows, 2 * HD), F32)
    return pl.pallas_call(
        attention_kernel,
        grid_spec=pltpu.PrefetchScalarGridSpec(
            num_scalar_prefetch=1,
            grid=(heads // PAIR,),
            in_specs=[pl.BlockSpec(slots[0].shape, whole)] * len(slots) + [pair] * 2,
            out_specs=[
                pair, pair, square, square, square,
                pl.BlockSpec((2, rows, 2 * HD), lambda h, place: (0, 0, 0)),
            ],
            scratch_shapes=[
                pltpu.VMEM((keys, HD), BF16),
                pltpu.VMEM((keys, HD), BF16),
                pltpu.VMEM((HD, keys), BF16),
                pltpu.VMEM((HD, keys), BF16),
                pltpu.VMEM((PAIR, keys, rows), F32),
                pltpu.VMEM((PAIR, keys, rows), BF16),
                pltpu.VMEM((PAIR, keys, rows), BF16),
                pltpu.VMEM((PAIR, keys, rows), F32),
                pltpu.VMEM((keys, 2 * HD), F32),
                pltpu.VMEM((8, rows), jnp.int32),
            ],
        ),
        out_shape=[
            jax.ShapeDtypeStruct((rows, width), BF16),
            jax.ShapeDtypeStruct((rows, width), BF16),
            part, part, part,
            jax.ShapeDtypeStruct((2, rows, 2 * HD), F32),
        ],
        compiler_params=pltpu.CompilerParams(vmem_limit_bytes=30 * MIB),
        cost_estimate=pl.CostEstimate(
            flops=12 * keys * width * rows, bytes_accessed=6 * MIB,
            transcendentals=keys * rows * heads,
        ),
    )(place, *slots, q, do)


def token(place, s, h, ring, few):
    return pl.multiple_of((lax.rem(place[3] + ring - s, ring) * 2 + h) * few, few)


def project_kernel(order, ring, last, place_ref, *refs):
    pieces, refs = refs[:len(order)], refs[len(order):]
    if last:
        wk_hbm, wv_hbm, seg_ref, early_ref, refs = *refs[:4], refs[6:]
    else:
        wk_hbm, wv_hbm, refs = *refs[:2], refs[2:]
    kv_ref, mine_hbm, theirs_hbm, h_ref, w_ref, come, come_w, go = refs
    few = pieces[0].shape[0]
    rows, width = h_ref.shape
    block = 2 * HD
    steps = come_w.shape[0] // 2
    depth = width // steps

    copies = [
        pltpu.make_async_copy(piece, h_ref.at[pl.ds(i * few, few), :], come.at[i])
        for i, piece in enumerate(pieces)
    ]
    weights = []
    for c in range(steps):
        at = pl.ds(c * depth, depth)
        weights.append([
            pltpu.make_async_copy(
                w.at[at, :], w_ref.at[at, pl.ds(i * HD, HD)], come_w.at[2 * c + i]
            )
            for i, w in enumerate((wk_hbm, wv_hbm))
        ])
    for copy in weights[0] + copies + sum(weights[1:], []):
        copy.start()
    for copy in copies:
        copy.wait()
    out = []
    base = 0 if not last else len(EARLY) * few
    for i in range(width // block):
        core, to = ((1 - place_ref[2], theirs_hbm), (place_ref[2], mine_hbm))[i % 2]
        first = pl.multiple_of((2 * (i // 2) + core) * block, block)
        out.append(pltpu.make_async_copy(
            h_ref.at[:, pl.ds(first, block)],
            to.at[pl.ds(base, rows), pl.ds(i // 2 * block, block)],
            go.at[i],
        ))
        out[-1].start()
    kv = jnp.zeros((rows, 2 * HD), F32)
    for c in range(steps):
        for copy in weights[c]:
            copy.wait()
        at = slice(c * depth, (c + 1) * depth)
        kv = kv + jnp.dot(h_ref[:, at], w_ref[at, :], preferred_element_type=F32)
    kv = kv.astype(BF16)
    if not last:
        kv_ref[...] = kv
    else:
        for i, (s, h) in enumerate(order):
            kv_ref[pl.ds(token(place_ref, s, h, ring, few), few), :] = kv[i * few:(i + 1) * few]
        for i, (s, h) in enumerate(EARLY):
            to = pl.ds(token(place_ref, s, h, ring, few), few)
            kv_ref[to, :] = early_ref[i * few:(i + 1) * few, :]
        total = seg_ref.shape[1]
        own = (seg_ref[...] + 1).astype(F32)
        kv_ref[total:, :] = jnp.broadcast_to(own, (kv_ref.shape[0] - total, total)).astype(BF16)
    for copy in out:
        copy.wait()


def project(place, order, pieces, key_weight, value_weight, ring, rest=()):
    few, width = pieces[0].shape
    rows = few * len(pieces)
    total = few * 2 * ring
    steps = 4
    far = pl.BlockSpec(memory_space=pl.ANY)
    whole = lambda i, place: (0, 0)
    kv_rows = total + 16 if rest else rows
    n = len(pieces)
    return pl.pallas_call(
        functools.partial(project_kernel, order, ring, bool(rest)),
        grid_spec=pltpu.PrefetchScalarGridSpec(
            num_scalar_prefetch=1,
            grid=(1,),
            in_specs=[far] * (n + 2)
            + ([pl.BlockSpec(a.shape, whole) for a in rest[:2]] + [far, far] if rest else []),
            out_specs=[pl.BlockSpec((kv_rows, 2 * HD), whole), far, far],
            scratch_shapes=[
                pltpu.VMEM((rows, width), BF16),
                pltpu.VMEM((width, 2 * HD), BF16),
                pltpu.SemaphoreType.DMA((n,)),
                pltpu.SemaphoreType.DMA((2 * steps,)),
                pltpu.SemaphoreType.DMA((width // (2 * HD),)),
            ],
        ),
        out_shape=[
            jax.ShapeDtypeStruct((kv_rows, 2 * HD), BF16),
            jax.ShapeDtypeStruct((total, width // 2), BF16),
            jax.ShapeDtypeStruct((total, width // 2), BF16),
        ],
        input_output_aliases={n + 5: 1, n + 6: 2} if rest else {},
        compiler_params=pltpu.CompilerParams(vmem_limit_bytes=VMEM),
        cost_estimate=pl.CostEstimate(
            flops=4 * rows * width * HD, bytes_accessed=8 * MIB, transcendentals=0
        ),
    )(place, *pieces, key_weight, value_weight, *rest)


def weight_grad_kernel(ring, place_ref, g_ref, gs_ref, *refs):
    hidden, (out_ref, grads_t, turn) = refs[:8], refs[8:]
    few = g_ref.shape[0] // (2 * ring)

    @pl.when(pl.program_id(0) == 0)
    def _():
        for p, g in enumerate((g_ref, gs_ref)):
            for i, (s, h) in enumerate(EARLY + LATE):
                turn[i * few:(i + 1) * few, :] = g[pl.ds(token(place_ref, s, h, ring, few), few), :]
            grads_t[p] = turn[...].T

    for i, (mine, other) in enumerate(zip(hidden[:4], hidden[4:])):
        out_ref[i] = (
            jnp.dot(grads_t[0], mine[...], preferred_element_type=F32)
            + jnp.dot(grads_t[1], other[...], preferred_element_type=F32)
        ).astype(BF16)


def weight_grad(place, grads, other_grads, mine, other, nx, ny, ring):
    rows, cols = grads.shape
    block = mine.shape[1] // (nx * ny)
    flat = pl.BlockSpec((rows, cols), lambda r, place: (0, 0))

    def column(i):
        return pl.BlockSpec((rows, block), lambda r, place: (0, r * ny + i))

    return pl.pallas_call(
        functools.partial(weight_grad_kernel, ring),
        grid_spec=pltpu.PrefetchScalarGridSpec(
            num_scalar_prefetch=1,
            grid=(nx,),
            in_specs=[flat, flat] + [column(i) for i in range(ny)] * 2,
            out_specs=pl.BlockSpec((ny, cols, block), lambda r, place: (r, 0, 0)),
            scratch_shapes=[pltpu.VMEM((2, cols, rows), BF16), pltpu.VMEM((rows, cols), BF16)],
        ),
        out_shape=jax.ShapeDtypeStruct((nx * ny, cols, block), BF16),
        compiler_params=pltpu.CompilerParams(vmem_limit_bytes=10 * MIB),
        cost_estimate=pl.CostEstimate(
            flops=4 * rows * cols * block * nx * ny, bytes_accessed=6 * MIB, transcendentals=0
        ),
    )(place, grads, other_grads, *[mine] * ny, *[other] * ny)


def finish_kernel(parts, key_ref, value_ref):
    total = parts[0].astype(F32)
    for i in range(1, parts.shape[0]):
        total = total + parts[i].astype(F32)
    key_ref[...] = total[:HD].T
    value_ref[...] = total[HD:].T


def finish(parts):
    _, cols, block = parts.shape
    half = pl.BlockSpec((block, HD), lambda i: (0, 0))
    shape = jax.ShapeDtypeStruct((block, HD), F32)
    return pl.pallas_call(
        finish_kernel,
        grid=(1,),
        in_specs=[pl.BlockSpec(parts.shape, lambda i: (0, 0, 0))],
        out_specs=[half, half],
        out_shape=[shape, shape],
        compiler_params=pltpu.CompilerParams(vmem_limit_bytes=8 * MIB),
    )(parts)


def spread_kernel(order, ring, place_ref, g_ref, wk_ref, wv_ref, *refs):
    outs, rows = refs[:-1], refs[-1]
    few = outs[0].shape[0]

    @pl.when(pl.program_id(0) == 0)
    def _():
        for i, (s, h) in enumerate(order):
            rows[i * few:(i + 1) * few, :] = g_ref[
                pl.ds(token(place_ref, ring - s, h, ring, few), few), :
            ]

    contract = (((1,), (1,)), ((), ()))
    part = lax.dot_general(
        rows[:, :HD], wk_ref[...], contract, preferred_element_type=F32
    ) + lax.dot_general(rows[:, HD:], wv_ref[...], contract, preferred_element_type=F32)
    for i, out in enumerate(outs):
        out[...] = part[i * few:(i + 1) * few].astype(BF16)


def spread(place, order, grads, key_weight, value_weight, ring):
    rows, cols = grads.shape
    few = rows // (2 * ring)
    width = key_weight.shape[0]
    tile = width // 8
    weight = pl.BlockSpec((tile, HD), lambda i, place: (i, 0))
    return pl.pallas_call(
        functools.partial(spread_kernel, order, ring),
        grid_spec=pltpu.PrefetchScalarGridSpec(
            num_scalar_prefetch=1,
            grid=(width // tile,),
            in_specs=[pl.BlockSpec((rows, cols), lambda i, place: (0, 0)), weight, weight],
            out_specs=[pl.BlockSpec((few, tile), lambda i, place: (0, i))] * len(order),
            scratch_shapes=[pltpu.VMEM((few * len(order), cols), BF16)],
        ),
        out_shape=[jax.ShapeDtypeStruct((few, width), BF16)] * len(order),
        compiler_params=pltpu.CompilerParams(vmem_limit_bytes=8 * MIB),
        cost_estimate=pl.CostEstimate(
            flops=2 * few * len(order) * cols * width, bytes_accessed=6 * MIB, transcendentals=0
        ),
    )(place, grads, key_weight, value_weight)


def on_device(hidden, key_weight, value_weight, queries, out_grad, segment_ids):
    rows = queries.shape[1]
    x_count, width = hidden.shape[1:]
    nx = lax.axis_size("dp")
    ny = lax.axis_size("y")
    heads = lax.axis_size("tp")
    x = lax.axis_index("dp")
    core = lax.axis_index("core")
    place = jnp.stack([x, lax.axis_index("y"), core, lax.axis_index("tp")]).astype(jnp.int32)
    swap = [(0, 1), (1, 0)]

    def swapped(a):
        return lax.ppermute(a, "core", swap)

    def shifted(a, s, axis="dp"):
        n = lax.axis_size(axis)
        return lax.ppermute(a, axis, [(i, (i + s) % n) for i in range(n)])

    half = x_count // 2
    ring = {(0, h): hidden[0, h * half:(h + 1) * half] for h in range(2)}
    for s in range(1, heads // 2 + 1):
        for h in range(2):
            if s < heads // 2 or h == 0:
                ring[s, h] = shifted(ring[s - 1, h], 1, "tp")
            if s < heads // 2 or h == 1:
                ring[heads - s, h] = shifted(ring[(heads - s + 1) % heads, h], -1, "tp")
    weights = (key_weight, value_weight)
    early = project(place, EARLY, [ring[i] for i in EARLY], *weights, heads)
    kv, mine, theirs = project(
        place, LATE, [ring[i] for i in LATE], *weights, heads, (segment_ids, *early)
    )

    down1 = [(i, i + 1) for i in range(ny - 1)]
    down2 = [(i, i + 2) for i in range(ny - 2)]
    kv1 = lax.ppermute(kv, "y", down1)
    kv2 = lax.ppermute(kv, "y", down2)
    near = lax.ppermute(kv, "core", [(0, 1)])
    kv3 = swapped(kv1)
    far = lax.ppermute(kv2, "core", [(1, 0)])

    att, dq, part0, part1, part2, part34 = attention(
        place, (kv, kv1, kv2, kv3, near, far), queries[0], out_grad[0]
    )

    up1 = [(i + 1, i) for i in range(ny - 1)]
    up2 = [(i + 2, i) for i in range(ny - 2)]
    got = swapped(part34)
    send1 = (part1 + got[0]).astype(BF16)
    send2 = (part2 + jnp.where(core == 0, 0.0, got[1])).astype(BF16)
    own = part0 + jnp.where(core == 0, got[1], 0.0)
    got1 = lax.ppermute(send1, "y", up1)
    got2 = lax.ppermute(send2, "y", up2)
    grads = (own + got1.astype(F32) + got2.astype(F32)).astype(BF16)

    other_grads = swapped(grads)
    part = dict(zip(FIRST, spread(place, FIRST, grads, *weights, heads)))
    other = swapped(theirs)
    grads, _ = lax.optimization_barrier((grads, part))
    sums = weight_grad(place, grads, other_grads, mine, other, nx, ny, heads)
    grads, sums = lax.optimization_barrier((grads, sums))
    key_wgrad, value_wgrad = finish(lax.all_to_all(sums, ("dp", "y"), 0, 0, tiled=True))

    part.update(zip(REST, spread(place, REST, grads, *weights, heads)))

    def travel(half, steps, by):
        moving = shifted(part[steps[0], half], by, "tp")
        for i, s in enumerate(steps[1:]):
            if i == 0:
                moving, _ = lax.optimization_barrier((moving, sums))
            moving = (moving.astype(F32) + part[s, half].astype(F32)).astype(BF16)
            moving = shifted(moving, by, "tp")
        return moving

    came = [
        travel(0, (4, 3, 2, 1), 1), travel(0, (5, 6, 7), -1),
        travel(1, (3, 2, 1), 1), travel(1, (4, 5, 6, 7), -1),
    ]
    came, key_wgrad, value_wgrad = lax.optimization_barrier((came, key_wgrad, value_wgrad))
    hidden_grad = jnp.concatenate([
        part[0, h].astype(F32) + came[2 * h].astype(F32) + came[2 * h + 1].astype(F32)
        for h in range(2)
    ]).astype(BF16)
    return (
        att[None],
        dq[None],
        hidden_grad[None],
        key_wgrad,
        value_wgrad,
    )


def solution(mesh):
    fine = Mesh(
        mesh.devices.reshape(mesh.shape["dp"], mesh.shape["ctx"] // 2, 2, mesh.shape["tp"]),
        ("dp", "y", "core", "tp"),
    )
    ctx = ("y", "core")
    in_specs = (
        P("dp", ("y", "core", "tp"), None),
        P(None, "tp"),
        P(None, "tp"),
        P("dp", ctx, "tp"),
        P("dp", ctx, "tp"),
        P("dp", ctx),
    )
    out_specs = (
        P("dp", ctx, "tp"),
        P("dp", ctx, "tp"),
        P("dp", ("y", "core", "tp"), None),
        P(("dp", "y", "core"), "tp"),
        P(("dp", "y", "core"), "tp"),
    )
    return jax.shard_map(
        on_device, mesh=fine, in_specs=in_specs, out_specs=out_specs, check_vma=False
    )
```

```python
import functools
import math

import jax
import jax.numpy as jnp
from jax import lax
from jax.experimental import pallas as pl
from jax.experimental.pallas import tpu as pltpu
from jax.sharding import Mesh, PartitionSpec as P

HD = 128
SLOTS = 5
PAIR = 4
EARLY = [(s, h) for s in (0, 1, 7, 2, 6) for h in (0, 1)] + [(3, 0), (5, 1)]
LATE = [(3, 1), (5, 0), (4, 0), (4, 1)]
FIRST = [(4, 0), (3, 1), (4, 1), (5, 0), (3, 0), (2, 1), (5, 1), (6, 0)]
REST = [(s, h) for s in range(8) for h in (0, 1) if (s, h) not in FIRST]
NEG = -1e30
MIB = 1024 * 1024
VMEM = 56 * MIB
F32 = jnp.float32
BF16 = jnp.bfloat16


def attention_kernel(place_ref, kv0, kv1, kv2, kv3, near, far, q_ref, do_ref,
                     att_ref, dq_ref, p0, p1, p2, p34,
                     k_all, v_all, kt_all, vt_all, s_ref, pb_ref, ds_ref, dp_ref, dkv_ref, thr_ref):
    rows = q_ref.shape[0]
    scale = 1.0 / math.sqrt(HD)
    log2e = math.log2(math.e)
    step = pl.program_id(0)
    heads = range(PAIR)
    spans = [pl.ds(j * rows, rows) for j in range(SLOTS)]

    @pl.when(step == 0)
    def _():
        blocks = (kv0[...], kv1[...], kv2[...], kv3[...], near[...] + far[...])
        documents = [kv[rows:, :].astype(F32) for kv in blocks]
        start = jnp.full((1, rows), (1 - SLOTS) * rows, jnp.int32)
        for doc in documents:
            earlier = doc.T[:, :1] < documents[0][:1, :]
            start = start + jnp.sum(earlier.astype(jnp.int32), axis=0, keepdims=True)
        core = place_ref[2]
        for j, back in enumerate((0, 2, 4, 1 + 2 * core, 3 - 2 * core)):
            thr_ref[j:j + 1, :] = start + back * rows
        for here, kv in zip(spans, blocks):
            k = kv[:rows, :HD]
            v = kv[:rows, HD:]
            k_all[here, :] = k
            v_all[here, :] = v
            kt_all[:, here] = k.T
            vt_all[:, here] = v.T
        dkv_ref[...] = jnp.zeros_like(dkv_ref)

    q = [q_ref[:, h * HD:(h + 1) * HD] for h in heads]
    do = [do_ref[:, h * HD:(h + 1) * HD] for h in heads]
    q_t = [a.T for a in q]
    do_t = [a.T for a in do]
    top = [jnp.full((1, rows), NEG, F32) for _ in heads]
    place = lax.broadcasted_iota(jnp.int32, (rows, rows), 0)
    for j, here in enumerate(spans):
        mask = place >= thr_ref[j:j + 1, :]
        if j == 0:
            mask = mask & (place <= lax.broadcasted_iota(jnp.int32, (rows, rows), 1))
        for h in heads:
            s = jnp.dot(k_all[here, :], q_t[h], preferred_element_type=F32)
            s = jnp.where(mask, s, NEG)
            s_ref[h, here, :] = s
            top[h] = jnp.maximum(top[h], jnp.max(s, axis=0, keepdims=True))
    total = [jnp.zeros((1, rows), F32) for _ in heads]
    for here in spans:
        for h in heads:
            e = jnp.exp2((s_ref[h, here, :] - top[h]) * (scale * log2e))
            s_ref[h, here, :] = e
            total[h] = total[h] + jnp.sum(e, axis=0, keepdims=True)
            dp_ref[h, here, :] = jnp.dot(v_all[here, :], do_t[h], preferred_element_type=F32)
    inv = [1.0 / t for t in total]
    for here in spans:
        for h in heads:
            pb_ref[h, here, :] = (s_ref[h, here, :] * inv[h]).astype(BF16)
    delta = []
    for h in heads:
        out_b = jnp.dot(vt_all[...], pb_ref[h], preferred_element_type=F32).astype(BF16)
        att_ref[:, h * HD:(h + 1) * HD] = out_b.T
        delta.append(jnp.sum(do_t[h].astype(F32) * out_b.astype(F32), axis=0, keepdims=True))
    for here in spans:
        dk = jnp.zeros((rows, HD), F32)
        dv = jnp.zeros((rows, HD), F32)
        for h in heads:
            ds = (s_ref[h, here, :] * inv[h] * (dp_ref[h, here, :] - delta[h])).astype(BF16)
            ds_ref[h, here, :] = ds
            dk = dk + jnp.dot(ds, q[h], preferred_element_type=F32)
            dv = dv + jnp.dot(pb_ref[h, here, :], do[h], preferred_element_type=F32)
        dkv_ref[here, :HD] += dk
        dkv_ref[here, HD:] += dv
    for h in heads:
        dq_t = jnp.dot(kt_all[...], ds_ref[h], preferred_element_type=F32)
        dq_ref[:, h * HD:(h + 1) * HD] = (dq_t * scale).astype(BF16).T

    @pl.when(step == pl.num_programs(0) - 1)
    def _():
        for here, out in zip(spans, (p0, p1, p2, p34.at[0], p34.at[1])):
            out[:, :HD] = dkv_ref[here, :HD] * scale
            out[:, HD:] = dkv_ref[here, HD:]


def attention(place, slots, q, do):
    rows, width = q.shape
    heads = width // HD
    keys = SLOTS * rows
    whole = lambda h, place: (0, 0)
    square = pl.BlockSpec((rows, 2 * HD), whole)
    pair = pl.BlockSpec((rows, PAIR * HD), lambda h, place: (0, h))
    part = jax.ShapeDtypeStruct((rows, 2 * HD), F32)
    return pl.pallas_call(
        attention_kernel,
        grid_spec=pltpu.PrefetchScalarGridSpec(
            num_scalar_prefetch=1,
            grid=(heads // PAIR,),
            in_specs=[pl.BlockSpec(slots[0].shape, whole)] * len(slots) + [pair] * 2,
            out_specs=[
                pair, pair, square, square, square,
                pl.BlockSpec((2, rows, 2 * HD), lambda h, place: (0, 0, 0)),
            ],
            scratch_shapes=[
                pltpu.VMEM((keys, HD), BF16),
                pltpu.VMEM((keys, HD), BF16),
                pltpu.VMEM((HD, keys), BF16),
                pltpu.VMEM((HD, keys), BF16),
                pltpu.VMEM((PAIR, keys, rows), F32),
                pltpu.VMEM((PAIR, keys, rows), BF16),
                pltpu.VMEM((PAIR, keys, rows), BF16),
                pltpu.VMEM((PAIR, keys, rows), F32),
                pltpu.VMEM((keys, 2 * HD), F32),
                pltpu.VMEM((8, rows), jnp.int32),
            ],
        ),
        out_shape=[
            jax.ShapeDtypeStruct((rows, width), BF16),
            jax.ShapeDtypeStruct((rows, width), BF16),
            part, part, part,
            jax.ShapeDtypeStruct((2, rows, 2 * HD), F32),
        ],
        compiler_params=pltpu.CompilerParams(vmem_limit_bytes=30 * MIB),
        cost_estimate=pl.CostEstimate(
            flops=12 * keys * width * rows, bytes_accessed=6 * MIB,
            transcendentals=keys * rows * heads,
        ),
    )(place, *slots, q, do)


def token(place, s, h, ring, few):
    return pl.multiple_of((lax.rem(place[3] + ring - s, ring) * 2 + h) * few, few)


def project_kernel(order, ring, last, place_ref, *refs):
    pieces, refs = refs[:len(order)], refs[len(order):]
    if last:
        wk_hbm, wv_hbm, seg_hbm, early_hbm, refs = *refs[:4], refs[6:]
        *refs, seg_ref, early_ref, come_rest = refs
    else:
        wk_hbm, wv_hbm, refs = *refs[:2], refs[2:]
    kv_ref, mine_hbm, theirs_hbm, h_ref, w_ref, come, come_w, go = refs
    few = pieces[0].shape[0]
    rows, width = h_ref.shape
    block = 2 * HD
    steps = come_w.shape[0] // 2
    depth = width // steps

    copies = [
        pltpu.make_async_copy(piece, h_ref.at[pl.ds(i * few, few), :], come.at[i])
        for i, piece in enumerate(pieces)
    ]
    weights = []
    for c in range(steps):
        at = pl.ds(c * depth, depth)
        weights.append([
            pltpu.make_async_copy(
                w.at[at, :], w_ref.at[at, pl.ds(i * HD, HD)], come_w.at[2 * c + i]
            )
            for i, w in enumerate((wk_hbm, wv_hbm))
        ])
    rest = []
    if last:
        rest = [
            pltpu.make_async_copy(seg_hbm, seg_ref, come_rest.at[0]),
            pltpu.make_async_copy(early_hbm, early_ref, come_rest.at[1]),
        ]
    for copy in weights[0] + copies + sum(weights[1:], []) + rest:
        copy.start()
    for copy in copies:
        copy.wait()
    out = []
    base = 0 if not last else len(EARLY) * few
    for i in range(width // block):
        core, to = ((1 - place_ref[2], theirs_hbm), (place_ref[2], mine_hbm))[i % 2]
        first = pl.multiple_of((2 * (i // 2) + core) * block, block)
        out.append(pltpu.make_async_copy(
            h_ref.at[:, pl.ds(first, block)],
            to.at[pl.ds(base, rows), pl.ds(i // 2 * block, block)],
            go.at[i],
        ))
        out[-1].start()
    kv = jnp.zeros((rows, 2 * HD), F32)
    for c in range(steps):
        for copy in weights[c]:
            copy.wait()
        at = slice(c * depth, (c + 1) * depth)
        kv = kv + jnp.dot(h_ref[:, at], w_ref[at, :], preferred_element_type=F32)
    kv = kv.astype(BF16)
    for copy in rest:
        copy.wait()
    if not last:
        kv_ref[...] = kv
    else:
        for i, (s, h) in enumerate(order):
            kv_ref[pl.ds(token(place_ref, s, h, ring, few), few), :] = kv[i * few:(i + 1) * few]
        for i, (s, h) in enumerate(EARLY):
            to = pl.ds(token(place_ref, s, h, ring, few), few)
            kv_ref[to, :] = early_ref[i * few:(i + 1) * few, :]
        total = seg_ref.shape[1]
        own = (seg_ref[...] + 1).astype(F32)
        kv_ref[total:, :] = jnp.broadcast_to(own, (kv_ref.shape[0] - total, total)).astype(BF16)
    for copy in out:
        copy.wait()


def project(place, order, pieces, key_weight, value_weight, ring, rest=()):
    few, width = pieces[0].shape
    rows = few * len(pieces)
    total = few * 2 * ring
    steps = 4
    far = pl.BlockSpec(memory_space=pl.ANY)
    whole = lambda i, place: (0, 0)
    kv_rows = total + 16 if rest else rows
    n = len(pieces)
    return pl.pallas_call(
        functools.partial(project_kernel, order, ring, bool(rest)),
        grid_spec=pltpu.PrefetchScalarGridSpec(
            num_scalar_prefetch=1,
            grid=(1,),
            in_specs=[far] * (n + 2)
            + [far] * len(rest),
            out_specs=[pl.BlockSpec((kv_rows, 2 * HD), whole), far, far],
            scratch_shapes=[
                pltpu.VMEM((rows, width), BF16),
                pltpu.VMEM((width, 2 * HD), BF16),
                pltpu.SemaphoreType.DMA((n,)),
                pltpu.SemaphoreType.DMA((2 * steps,)),
                pltpu.SemaphoreType.DMA((width // (2 * HD),)),
            ]
            + ([pltpu.VMEM(a.shape, a.dtype) for a in rest[:2]] if rest else [])
            + ([pltpu.SemaphoreType.DMA((2,))] if rest else []),
        ),
        out_shape=[
            jax.ShapeDtypeStruct((kv_rows, 2 * HD), BF16),
            jax.ShapeDtypeStruct((total, width // 2), BF16),
            jax.ShapeDtypeStruct((total, width // 2), BF16),
        ],
        input_output_aliases={n + 5: 1, n + 6: 2} if rest else {},
        compiler_params=pltpu.CompilerParams(vmem_limit_bytes=VMEM),
        cost_estimate=pl.CostEstimate(
            flops=4 * rows * width * HD, bytes_accessed=8 * MIB, transcendentals=0
        ),
    )(place, *pieces, key_weight, value_weight, *rest)


def weight_grad_kernel(ring, place_ref, g_ref, gs_ref, *refs):
    hidden, (out_ref, grads_t, turn) = refs[:8], refs[8:]
    few = g_ref.shape[0] // (2 * ring)

    @pl.when(pl.program_id(0) == 0)
    def _():
        for p, g in enumerate((g_ref, gs_ref)):
            for i, (s, h) in enumerate(EARLY + LATE):
                turn[i * few:(i + 1) * few, :] = g[pl.ds(token(place_ref, s, h, ring, few), few), :]
            grads_t[p] = turn[...].T

    for i, (mine, other) in enumerate(zip(hidden[:4], hidden[4:])):
        out_ref[i] = (
            jnp.dot(grads_t[0], mine[...], preferred_element_type=F32)
            + jnp.dot(grads_t[1], other[...], preferred_element_type=F32)
        ).astype(BF16)


def weight_grad(place, grads, other_grads, mine, other, nx, ny, ring):
    rows, cols = grads.shape
    block = mine.shape[1] // (nx * ny)
    flat = pl.BlockSpec((rows, cols), lambda r, place: (0, 0))

    def column(i):
        return pl.BlockSpec((rows, block), lambda r, place: (0, r * ny + i))

    return pl.pallas_call(
        functools.partial(weight_grad_kernel, ring),
        grid_spec=pltpu.PrefetchScalarGridSpec(
            num_scalar_prefetch=1,
            grid=(nx,),
            in_specs=[flat, flat] + [column(i) for i in range(ny)] * 2,
            out_specs=pl.BlockSpec((ny, cols, block), lambda r, place: (r, 0, 0)),
            scratch_shapes=[pltpu.VMEM((2, cols, rows), BF16), pltpu.VMEM((rows, cols), BF16)],
        ),
        out_shape=jax.ShapeDtypeStruct((nx * ny, cols, block), BF16),
        compiler_params=pltpu.CompilerParams(vmem_limit_bytes=10 * MIB),
        cost_estimate=pl.CostEstimate(
            flops=4 * rows * cols * block * nx * ny, bytes_accessed=6 * MIB, transcendentals=0
        ),
    )(place, grads, other_grads, *[mine] * ny, *[other] * ny)


def finish_kernel(parts, key_ref, value_ref):
    total = parts[0].astype(F32)
    for i in range(1, parts.shape[0]):
        total = total + parts[i].astype(F32)
    key_ref[...] = total[:HD].T
    value_ref[...] = total[HD:].T


def finish(parts):
    _, cols, block = parts.shape
    half = pl.BlockSpec((block, HD), lambda i: (0, 0))
    shape = jax.ShapeDtypeStruct((block, HD), F32)
    return pl.pallas_call(
        finish_kernel,
        grid=(1,),
        in_specs=[pl.BlockSpec(parts.shape, lambda i: (0, 0, 0))],
        out_specs=[half, half],
        out_shape=[shape, shape],
        compiler_params=pltpu.CompilerParams(vmem_limit_bytes=8 * MIB),
    )(parts)


def spread_kernel(order, ring, place_ref, g_ref, wk_ref, wv_ref, *refs):
    outs, rows = refs[:-1], refs[-1]
    few = outs[0].shape[0]

    @pl.when(pl.program_id(0) == 0)
    def _():
        for i, (s, h) in enumerate(order):
            rows[i * few:(i + 1) * few, :] = g_ref[
                pl.ds(token(place_ref, ring - s, h, ring, few), few), :
            ]

    contract = (((1,), (1,)), ((), ()))
    part = lax.dot_general(
        rows[:, :HD], wk_ref[...], contract, preferred_element_type=F32
    ) + lax.dot_general(rows[:, HD:], wv_ref[...], contract, preferred_element_type=F32)
    for i, out in enumerate(outs):
        out[...] = part[i * few:(i + 1) * few].astype(BF16)


def spread(place, order, grads, key_weight, value_weight, ring):
    rows, cols = grads.shape
    few = rows // (2 * ring)
    width = key_weight.shape[0]
    tile = width // 8
    weight = pl.BlockSpec((tile, HD), lambda i, place: (i, 0))
    return pl.pallas_call(
        functools.partial(spread_kernel, order, ring),
        grid_spec=pltpu.PrefetchScalarGridSpec(
            num_scalar_prefetch=1,
            grid=(width // tile,),
            in_specs=[pl.BlockSpec((rows, cols), lambda i, place: (0, 0)), weight, weight],
            out_specs=[pl.BlockSpec((few, tile), lambda i, place: (0, i))] * len(order),
            scratch_shapes=[pltpu.VMEM((few * len(order), cols), BF16)],
        ),
        out_shape=[jax.ShapeDtypeStruct((few, width), BF16)] * len(order),
        compiler_params=pltpu.CompilerParams(vmem_limit_bytes=8 * MIB),
        cost_estimate=pl.CostEstimate(
            flops=2 * few * len(order) * cols * width, bytes_accessed=6 * MIB, transcendentals=0
        ),
    )(place, grads, key_weight, value_weight)


def on_device(hidden, key_weight, value_weight, queries, out_grad, segment_ids):
    rows = queries.shape[1]
    x_count, width = hidden.shape[1:]
    nx = lax.axis_size("dp")
    ny = lax.axis_size("y")
    heads = lax.axis_size("tp")
    x = lax.axis_index("dp")
    core = lax.axis_index("core")
    place = jnp.stack([x, lax.axis_index("y"), core, lax.axis_index("tp")]).astype(jnp.int32)
    swap = [(0, 1), (1, 0)]

    def swapped(a):
        return lax.ppermute(a, "core", swap)

    def shifted(a, s, axis="dp"):
        n = lax.axis_size(axis)
        return lax.ppermute(a, axis, [(i, (i + s) % n) for i in range(n)])

    half = x_count // 2
    ring = {(0, h): hidden[0, h * half:(h + 1) * half] for h in range(2)}
    for s in range(1, heads // 2 + 1):
        for h in range(2):
            if s < heads // 2 or h == 0:
                ring[s, h] = shifted(ring[s - 1, h], 1, "tp")
            if s < heads // 2 or h == 1:
                ring[heads - s, h] = shifted(ring[(heads - s + 1) % heads, h], -1, "tp")
    weights = (key_weight, value_weight)
    early = project(place, EARLY, [ring[i] for i in EARLY], *weights, heads)
    kv, mine, theirs = project(
        place, LATE, [ring[i] for i in LATE], *weights, heads, (segment_ids, *early)
    )

    down1 = [(i, i + 1) for i in range(ny - 1)]
    down2 = [(i, i + 2) for i in range(ny - 2)]
    kv1 = lax.ppermute(kv, "y", down1)
    kv2 = lax.ppermute(kv, "y", down2)
    near = lax.ppermute(kv, "core", [(0, 1)])
    kv3 = swapped(kv1)
    far = lax.ppermute(kv2, "core", [(1, 0)])

    att, dq, part0, part1, part2, part34 = attention(
        place, (kv, kv1, kv2, kv3, near, far), queries[0], out_grad[0]
    )

    up1 = [(i + 1, i) for i in range(ny - 1)]
    up2 = [(i + 2, i) for i in range(ny - 2)]
    got = swapped(part34)
    send1 = (part1 + got[0]).astype(BF16)
    send2 = (part2 + jnp.where(core == 0, 0.0, got[1])).astype(BF16)
    own = part0 + jnp.where(core == 0, got[1], 0.0)
    got1 = lax.ppermute(send1, "y", up1)
    got2 = lax.ppermute(send2, "y", up2)
    grads = (own + got1.astype(F32) + got2.astype(F32)).astype(BF16)

    other_grads = swapped(grads)
    part = dict(zip(FIRST, spread(place, FIRST, grads, *weights, heads)))
    other = swapped(theirs)
    grads, _ = lax.optimization_barrier((grads, part))
    sums = weight_grad(place, grads, other_grads, mine, other, nx, ny, heads)
    grads, sums = lax.optimization_barrier((grads, sums))
    part.update(zip(REST, spread(place, REST, grads, *weights, heads)))

    def joined(moving, s, half):
        return (moving.astype(F32) + part[s, half].astype(F32)).astype(BF16)

    routes = [
        (0, (4, 3, 2, 1), 1), (1, (4, 5, 6, 7), -1), (1, (3, 2, 1), 1), (0, (5, 6, 7), -1)
    ]
    came = [shifted(part[steps[0], half], by, "tp") for half, steps, by in routes]
    sums, *came[:2] = lax.optimization_barrier((sums, *came[:2]))
    came[:2] = [joined(moving, steps[1], half) for moving, (half, steps, _) in zip(came, routes[:2])]
    sums, *came[:2] = lax.optimization_barrier((sums, *came[:2]))
    _, *came[2:] = lax.optimization_barrier((came[0], *came[2:]))
    came[2:] = [joined(moving, steps[1], half) for moving, (half, steps, _) in zip(came[2:], routes[2:])]
    key_wgrad, value_wgrad = finish(lax.all_to_all(sums, ("dp", "y"), 0, 0, tiled=True))
    for i, (half, steps, by) in enumerate(routes):
        moving = shifted(came[i], by, "tp")
        for s in steps[2:]:
            moving = shifted(joined(moving, s, half), by, "tp")
        came[i] = moving
    came, key_wgrad, value_wgrad = lax.optimization_barrier((came, key_wgrad, value_wgrad))
    hidden_grad = jnp.concatenate([
        part[0, h].astype(F32) + came[h].astype(F32) + came[3 - h].astype(F32)
        for h in range(2)
    ]).astype(BF16)
    return (
        att[None],
        dq[None],
        hidden_grad[None],
        key_wgrad,
        value_wgrad,
    )


def solution(mesh):
    fine = Mesh(
        mesh.devices.reshape(mesh.shape["dp"], mesh.shape["ctx"] // 2, 2, mesh.shape["tp"]),
        ("dp", "y", "core", "tp"),
    )
    ctx = ("y", "core")
    in_specs = (
        P("dp", ("y", "core", "tp"), None),
        P(None, "tp"),
        P(None, "tp"),
        P("dp", ctx, "tp"),
        P("dp", ctx, "tp"),
        P("dp", ctx),
    )
    out_specs = (
        P("dp", ctx, "tp"),
        P("dp", ctx, "tp"),
        P("dp", ("y", "core", "tp"), None),
        P(("dp", "y", "core"), "tp"),
        P(("dp", "y", "core"), "tp"),
    )
    return jax.shard_map(
        on_device, mesh=fine, in_specs=in_specs, out_specs=out_specs, check_vma=False
    )
```

```python
import functools
import math

import jax
import jax.numpy as jnp
from jax import lax
from jax.experimental import pallas as pl
from jax.experimental.pallas import tpu as pltpu
from jax.sharding import Mesh, PartitionSpec as P

HD = 128
SLOTS = 5
PAIR = 4
EARLY = [(s, h) for s in (0, 1, 7, 2, 6) for h in (0, 1)] + [(3, 0), (5, 1)]
LATE = [(3, 1), (5, 0), (4, 0), (4, 1)]
FIRST = [(4, 0), (3, 1), (4, 1), (5, 0), (3, 0), (2, 1), (5, 1), (6, 0)]
REST = [(s, h) for s in range(8) for h in (0, 1) if (s, h) not in FIRST]
NEG = -1e30
MIB = 1024 * 1024
VMEM = 56 * MIB
F32 = jnp.float32
BF16 = jnp.bfloat16


def attention_kernel(place_ref, kv0, kv1, kv2, kv3, near, far, q_ref, do_ref,
                     att_ref, dq_ref, p0, p1, p2, p34,
                     k_all, v_all, kt_all, vt_all, s_ref, pb_ref, ds_ref, dp_ref, dkv_ref, thr_ref):
    rows = q_ref.shape[0]
    scale = 1.0 / math.sqrt(HD)
    log2e = math.log2(math.e)
    step = pl.program_id(0)
    heads = range(PAIR)
    spans = [pl.ds(j * rows, rows) for j in range(SLOTS)]

    @pl.when(step == 0)
    def _():
        blocks = (kv0[...], kv1[...], kv2[...], kv3[...], near[...] + far[...])
        documents = [kv[rows:, :].astype(F32) for kv in blocks]
        start = jnp.full((1, rows), (1 - SLOTS) * rows, jnp.int32)
        for doc in documents:
            earlier = doc.T[:, :1] < documents[0][:1, :]
            start = start + jnp.sum(earlier.astype(jnp.int32), axis=0, keepdims=True)
        core = place_ref[2]
        for j, back in enumerate((0, 2, 4, 1 + 2 * core, 3 - 2 * core)):
            thr_ref[j:j + 1, :] = start + back * rows
        for here, kv in zip(spans, blocks):
            k = kv[:rows, :HD]
            v = kv[:rows, HD:]
            k_all[here, :] = k
            v_all[here, :] = v
            kt_all[:, here] = k.T
            vt_all[:, here] = v.T
        dkv_ref[...] = jnp.zeros_like(dkv_ref)

    q = [q_ref[:, h * HD:(h + 1) * HD] for h in heads]
    do = [do_ref[:, h * HD:(h + 1) * HD] for h in heads]
    q_t = [a.T for a in q]
    do_t = [a.T for a in do]
    top = [jnp.full((1, rows), NEG, F32) for _ in heads]
    place = lax.broadcasted_iota(jnp.int32, (rows, rows), 0)
    for j, here in enumerate(spans):
        mask = place >= thr_ref[j:j + 1, :]
        if j == 0:
            mask = mask & (place <= lax.broadcasted_iota(jnp.int32, (rows, rows), 1))
        for h in heads:
            s = jnp.dot(k_all[here, :], q_t[h], preferred_element_type=F32)
            s = jnp.where(mask, s, NEG)
            s_ref[h, here, :] = s
            top[h] = jnp.maximum(top[h], jnp.max(s, axis=0, keepdims=True))
    total = [jnp.zeros((1, rows), F32) for _ in heads]
    for here in spans:
        for h in heads:
            e = jnp.exp2((s_ref[h, here, :] - top[h]) * (scale * log2e))
            s_ref[h, here, :] = e
            total[h] = total[h] + jnp.sum(e, axis=0, keepdims=True)
            dp_ref[h, here, :] = jnp.dot(v_all[here, :], do_t[h], preferred_element_type=F32)
    inv = [1.0 / t for t in total]
    for here in spans:
        for h in heads:
            pb_ref[h, here, :] = (s_ref[h, here, :] * inv[h]).astype(BF16)
    delta = []
    for h in heads:
        out_b = jnp.dot(vt_all[...], pb_ref[h], preferred_element_type=F32).astype(BF16)
        att_ref[:, h * HD:(h + 1) * HD] = out_b.T
        delta.append(jnp.sum(do_t[h].astype(F32) * out_b.astype(F32), axis=0, keepdims=True))
    for here in spans:
        dk = jnp.zeros((rows, HD), F32)
        dv = jnp.zeros((rows, HD), F32)
        for h in heads:
            ds = (s_ref[h, here, :] * inv[h] * (dp_ref[h, here, :] - delta[h])).astype(BF16)
            ds_ref[h, here, :] = ds
            dk = dk + jnp.dot(ds, q[h], preferred_element_type=F32)
            dv = dv + jnp.dot(pb_ref[h, here, :], do[h], preferred_element_type=F32)
        dkv_ref[here, :HD] += dk
        dkv_ref[here, HD:] += dv
    for h in heads:
        dq_t = jnp.dot(kt_all[...], ds_ref[h], preferred_element_type=F32)
        dq_ref[:, h * HD:(h + 1) * HD] = (dq_t * scale).astype(BF16).T

    @pl.when(step == pl.num_programs(0) - 1)
    def _():
        for here, out in zip(spans, (p0, p1, p2, p34.at[0], p34.at[1])):
            out[:, :HD] = dkv_ref[here, :HD] * scale
            out[:, HD:] = dkv_ref[here, HD:]


def attention(place, slots, q, do):
    rows, width = q.shape
    heads = width // HD
    keys = SLOTS * rows
    whole = lambda h, place: (0, 0)
    square = pl.BlockSpec((rows, 2 * HD), whole)
    pair = pl.BlockSpec((rows, PAIR * HD), lambda h, place: (0, h))
    part = jax.ShapeDtypeStruct((rows, 2 * HD), F32)
    return pl.pallas_call(
        attention_kernel,
        grid_spec=pltpu.PrefetchScalarGridSpec(
            num_scalar_prefetch=1,
            grid=(heads // PAIR,),
            in_specs=[pl.BlockSpec(slots[0].shape, whole)] * len(slots) + [pair] * 2,
            out_specs=[
                pair, pair, square, square, square,
                pl.BlockSpec((2, rows, 2 * HD), lambda h, place: (0, 0, 0)),
            ],
            scratch_shapes=[
                pltpu.VMEM((keys, HD), BF16),
                pltpu.VMEM((keys, HD), BF16),
                pltpu.VMEM((HD, keys), BF16),
                pltpu.VMEM((HD, keys), BF16),
                pltpu.VMEM((PAIR, keys, rows), F32),
                pltpu.VMEM((PAIR, keys, rows), BF16),
                pltpu.VMEM((PAIR, keys, rows), BF16),
                pltpu.VMEM((PAIR, keys, rows), F32),
                pltpu.VMEM((keys, 2 * HD), F32),
                pltpu.VMEM((8, rows), jnp.int32),
            ],
        ),
        out_shape=[
            jax.ShapeDtypeStruct((rows, width), BF16),
            jax.ShapeDtypeStruct((rows, width), BF16),
            part, part, part,
            jax.ShapeDtypeStruct((2, rows, 2 * HD), F32),
        ],
        compiler_params=pltpu.CompilerParams(vmem_limit_bytes=30 * MIB),
        cost_estimate=pl.CostEstimate(
            flops=12 * keys * width * rows, bytes_accessed=6 * MIB,
            transcendentals=keys * rows * heads,
        ),
    )(place, *slots, q, do)


def token(place, s, h, ring, few):
    return pl.multiple_of((lax.rem(place[3] + ring - s, ring) * 2 + h) * few, few)


def project_kernel(order, ring, last, place_ref, *refs):
    pieces, refs = refs[:len(order)], refs[len(order):]
    if last:
        wk_hbm, wv_hbm, seg_hbm, early_hbm, refs = *refs[:4], refs[6:]
        *refs, seg_ref, early_ref, come_rest = refs
    else:
        wk_hbm, wv_hbm, refs = *refs[:2], refs[2:]
    kv_ref, mine_hbm, theirs_hbm, h_ref, w_ref, come, come_w, go = refs
    few = pieces[0].shape[0]
    rows, width = h_ref.shape
    block = 2 * HD
    steps = come_w.shape[0] // 2
    depth = width // steps

    copies = [
        pltpu.make_async_copy(piece, h_ref.at[pl.ds(i * few, few), :], come.at[i])
        for i, piece in enumerate(pieces)
    ]
    weights = []
    for c in range(steps):
        at = pl.ds(c * depth, depth)
        weights.append([
            pltpu.make_async_copy(
                w.at[at, :], w_ref.at[at, pl.ds(i * HD, HD)], come_w.at[2 * c + i]
            )
            for i, w in enumerate((wk_hbm, wv_hbm))
        ])
    rest = []
    if last:
        rest = [
            pltpu.make_async_copy(seg_hbm, seg_ref, come_rest.at[0]),
            pltpu.make_async_copy(early_hbm, early_ref, come_rest.at[1]),
        ]
    for copy in weights[0] + copies + sum(weights[1:], []) + rest:
        copy.start()
    for copy in copies:
        copy.wait()
    out = []
    base = 0 if not last else len(EARLY) * few
    for i in range(width // block):
        core, to = ((1 - place_ref[2], theirs_hbm), (place_ref[2], mine_hbm))[i % 2]
        first = pl.multiple_of((2 * (i // 2) + core) * block, block)
        out.append(pltpu.make_async_copy(
            h_ref.at[:, pl.ds(first, block)],
            to.at[pl.ds(base, rows), pl.ds(i // 2 * block, block)],
            go.at[i],
        ))
        out[-1].start()
    kv = jnp.zeros((rows, 2 * HD), F32)
    for c in range(steps):
        for copy in weights[c]:
            copy.wait()
        at = slice(c * depth, (c + 1) * depth)
        kv = kv + jnp.dot(h_ref[:, at], w_ref[at, :], preferred_element_type=F32)
    kv = kv.astype(BF16)
    for copy in rest:
        copy.wait()
    if not last:
        kv_ref[...] = kv
    else:
        for i, (s, h) in enumerate(order):
            kv_ref[pl.ds(token(place_ref, s, h, ring, few), few), :] = kv[i * few:(i + 1) * few]
        for i, (s, h) in enumerate(EARLY):
            to = pl.ds(token(place_ref, s, h, ring, few), few)
            kv_ref[to, :] = early_ref[i * few:(i + 1) * few, :]
        total = seg_ref.shape[1]
        own = (seg_ref[...] + 1).astype(F32)
        kv_ref[total:, :] = jnp.broadcast_to(own, (kv_ref.shape[0] - total, total)).astype(BF16)
    for copy in out:
        copy.wait()


def project(place, order, pieces, key_weight, value_weight, ring, rest=()):
    few, width = pieces[0].shape
    rows = few * len(pieces)
    total = few * 2 * ring
    steps = 4
    far = pl.BlockSpec(memory_space=pl.ANY)
    whole = lambda i, place: (0, 0)
    kv_rows = total + 16 if rest else rows
    n = len(pieces)
    return pl.pallas_call(
        functools.partial(project_kernel, order, ring, bool(rest)),
        grid_spec=pltpu.PrefetchScalarGridSpec(
            num_scalar_prefetch=1,
            grid=(1,),
            in_specs=[far] * (n + 2)
            + [far] * len(rest),
            out_specs=[pl.BlockSpec((kv_rows, 2 * HD), whole), far, far],
            scratch_shapes=[
                pltpu.VMEM((rows, width), BF16),
                pltpu.VMEM((width, 2 * HD), BF16),
                pltpu.SemaphoreType.DMA((n,)),
                pltpu.SemaphoreType.DMA((2 * steps,)),
                pltpu.SemaphoreType.DMA((width // (2 * HD),)),
            ]
            + ([pltpu.VMEM(a.shape, a.dtype) for a in rest[:2]] if rest else [])
            + ([pltpu.SemaphoreType.DMA((2,))] if rest else []),
        ),
        out_shape=[
            jax.ShapeDtypeStruct((kv_rows, 2 * HD), BF16),
            jax.ShapeDtypeStruct((total, width // 2), BF16),
            jax.ShapeDtypeStruct((total, width // 2), BF16),
        ],
        input_output_aliases={n + 5: 1, n + 6: 2} if rest else {},
        compiler_params=pltpu.CompilerParams(vmem_limit_bytes=VMEM),
        cost_estimate=pl.CostEstimate(
            flops=4 * rows * width * HD, bytes_accessed=8 * MIB, transcendentals=0
        ),
    )(place, *pieces, key_weight, value_weight, *rest)


def weight_grad_kernel(ring, place_ref, g_ref, gs_ref, *refs):
    hidden, (out_ref, grads_t, turn) = refs[:8], refs[8:]
    few = g_ref.shape[0] // (2 * ring)

    @pl.when(pl.program_id(0) == 0)
    def _():
        for p, g in enumerate((g_ref, gs_ref)):
            for i, (s, h) in enumerate(EARLY + LATE):
                turn[i * few:(i + 1) * few, :] = g[pl.ds(token(place_ref, s, h, ring, few), few), :]
            grads_t[p] = turn[...].T

    for i, (mine, other) in enumerate(zip(hidden[:4], hidden[4:])):
        out_ref[i] = (
            jnp.dot(grads_t[0], mine[...], preferred_element_type=F32)
            + jnp.dot(grads_t[1], other[...], preferred_element_type=F32)
        ).astype(BF16)


def weight_grad(place, grads, other_grads, mine, other, nx, ny, ring):
    rows, cols = grads.shape
    block = mine.shape[1] // (nx * ny)
    flat = pl.BlockSpec((rows, cols), lambda r, place: (0, 0))

    def column(i):
        return pl.BlockSpec((rows, block), lambda r, place: (0, r * ny + i))

    return pl.pallas_call(
        functools.partial(weight_grad_kernel, ring),
        grid_spec=pltpu.PrefetchScalarGridSpec(
            num_scalar_prefetch=1,
            grid=(nx,),
            in_specs=[flat, flat] + [column(i) for i in range(ny)] * 2,
            out_specs=pl.BlockSpec((ny, cols, block), lambda r, place: (r, 0, 0)),
            scratch_shapes=[pltpu.VMEM((2, cols, rows), BF16), pltpu.VMEM((rows, cols), BF16)],
        ),
        out_shape=jax.ShapeDtypeStruct((nx * ny, cols, block), BF16),
        compiler_params=pltpu.CompilerParams(vmem_limit_bytes=10 * MIB),
        cost_estimate=pl.CostEstimate(
            flops=4 * rows * cols * block * nx * ny, bytes_accessed=6 * MIB, transcendentals=0
        ),
    )(place, grads, other_grads, *[mine] * ny, *[other] * ny)


def finish_kernel(parts, key_ref, value_ref):
    total = parts[0].astype(F32)
    for i in range(1, parts.shape[0]):
        total = total + parts[i].astype(F32)
    key_ref[...] = total[:HD].T
    value_ref[...] = total[HD:].T


def finish(parts):
    _, cols, block = parts.shape
    n = parts.shape[0]
    half = pl.BlockSpec((block // 2, HD), lambda i: (i, 0))
    shape = jax.ShapeDtypeStruct((block, HD), F32)
    return pl.pallas_call(
        finish_kernel,
        grid=(2,),
        in_specs=[pl.BlockSpec((n, cols, block // 2), lambda i: (0, 0, i))],
        out_specs=[half, half],
        out_shape=[shape, shape],
        compiler_params=pltpu.CompilerParams(vmem_limit_bytes=8 * MIB),
    )(parts)


def spread_kernel(order, ring, place_ref, g_ref, wk_ref, wv_ref, *refs):
    outs, rows = refs[:-1], refs[-1]
    few = outs[0].shape[0]

    @pl.when(pl.program_id(0) == 0)
    def _():
        for i, (s, h) in enumerate(order):
            rows[i * few:(i + 1) * few, :] = g_ref[
                pl.ds(token(place_ref, ring - s, h, ring, few), few), :
            ]

    contract = (((1,), (1,)), ((), ()))
    part = lax.dot_general(
        rows[:, :HD], wk_ref[...], contract, preferred_element_type=F32
    ) + lax.dot_general(rows[:, HD:], wv_ref[...], contract, preferred_element_type=F32)
    for i, out in enumerate(outs):
        out[...] = part[i * few:(i + 1) * few].astype(BF16)


def spread(place, order, grads, key_weight, value_weight, ring):
    rows, cols = grads.shape
    few = rows // (2 * ring)
    width = key_weight.shape[0]
    tile = width // 8
    weight = pl.BlockSpec((tile, HD), lambda i, place: (i, 0))
    return pl.pallas_call(
        functools.partial(spread_kernel, order, ring),
        grid_spec=pltpu.PrefetchScalarGridSpec(
            num_scalar_prefetch=1,
            grid=(width // tile,),
            in_specs=[pl.BlockSpec((rows, cols), lambda i, place: (0, 0)), weight, weight],
            out_specs=[pl.BlockSpec((few, tile), lambda i, place: (0, i))] * len(order),
            scratch_shapes=[pltpu.VMEM((few * len(order), cols), BF16)],
        ),
        out_shape=[jax.ShapeDtypeStruct((few, width), BF16)] * len(order),
        compiler_params=pltpu.CompilerParams(vmem_limit_bytes=8 * MIB),
        cost_estimate=pl.CostEstimate(
            flops=2 * few * len(order) * cols * width, bytes_accessed=6 * MIB, transcendentals=0
        ),
    )(place, grads, key_weight, value_weight)


def on_device(hidden, key_weight, value_weight, queries, out_grad, segment_ids):
    rows = queries.shape[1]
    x_count, width = hidden.shape[1:]
    nx = lax.axis_size("dp")
    ny = lax.axis_size("y")
    heads = lax.axis_size("tp")
    x = lax.axis_index("dp")
    core = lax.axis_index("core")
    place = jnp.stack([x, lax.axis_index("y"), core, lax.axis_index("tp")]).astype(jnp.int32)
    swap = [(0, 1), (1, 0)]

    def swapped(a):
        return lax.ppermute(a, "core", swap)

    def shifted(a, s, axis="dp"):
        n = lax.axis_size(axis)
        return lax.ppermute(a, axis, [(i, (i + s) % n) for i in range(n)])

    half = x_count // 2
    ring = {(0, h): hidden[0, h * half:(h + 1) * half] for h in range(2)}
    for s in range(1, heads // 2 + 1):
        for h in range(2):
            if s < heads // 2 or h == 0:
                ring[s, h] = shifted(ring[s - 1, h], 1, "tp")
            if s < heads // 2 or h == 1:
                ring[heads - s, h] = shifted(ring[(heads - s + 1) % heads, h], -1, "tp")
    weights = (key_weight, value_weight)
    early = project(place, EARLY, [ring[i] for i in EARLY], *weights, heads)
    kv, mine, theirs = project(
        place, LATE, [ring[i] for i in LATE], *weights, heads, (segment_ids, *early)
    )

    down1 = [(i, i + 1) for i in range(ny - 1)]
    down2 = [(i, i + 2) for i in range(ny - 2)]
    kv1 = lax.ppermute(kv, "y", down1)
    kv2 = lax.ppermute(kv, "y", down2)
    near = lax.ppermute(kv, "core", [(0, 1)])
    kv3 = swapped(kv1)
    far = lax.ppermute(kv2, "core", [(1, 0)])

    att, dq, part0, part1, part2, part34 = attention(
        place, (kv, kv1, kv2, kv3, near, far), queries[0], out_grad[0]
    )

    up1 = [(i + 1, i) for i in range(ny - 1)]
    up2 = [(i + 2, i) for i in range(ny - 2)]
    got = swapped(part34)
    send1 = (part1 + got[0]).astype(BF16)
    send2 = (part2 + jnp.where(core == 0, 0.0, got[1])).astype(BF16)
    own = part0 + jnp.where(core == 0, got[1], 0.0)
    got1 = lax.ppermute(send1, "y", up1)
    got2 = lax.ppermute(send2, "y", up2)
    grads = (own + got1.astype(F32) + got2.astype(F32)).astype(BF16)

    other_grads = swapped(grads)
    part = dict(zip(FIRST, spread(place, FIRST, grads, *weights, heads)))
    other = swapped(theirs)
    grads, _ = lax.optimization_barrier((grads, part))
    sums = weight_grad(place, grads, other_grads, mine, other, nx, ny, heads)
    grads, sums = lax.optimization_barrier((grads, sums))
    part.update(zip(REST, spread(place, REST, grads, *weights, heads)))

    def joined(moving, s, half):
        return (moving.astype(F32) + part[s, half].astype(F32)).astype(BF16)

    routes = [
        (0, (4, 3, 2, 1), 1), (1, (4, 5, 6, 7), -1), (1, (3, 2, 1), 1), (0, (5, 6, 7), -1)
    ]
    came = [shifted(part[steps[0], half], by, "tp") for half, steps, by in routes]
    sums, *came[:2] = lax.optimization_barrier((sums, *came[:2]))
    came[:2] = [joined(moving, steps[1], half) for moving, (half, steps, _) in zip(came, routes[:2])]
    sums, *came[:2] = lax.optimization_barrier((sums, *came[:2]))
    _, *came[2:] = lax.optimization_barrier((came[0], *came[2:]))
    came[2:] = [joined(moving, steps[1], half) for moving, (half, steps, _) in zip(came[2:], routes[2:])]
    key_wgrad, value_wgrad = finish(lax.all_to_all(sums, ("dp", "y"), 0, 0, tiled=True))
    for i, (half, steps, by) in enumerate(routes):
        moving = shifted(came[i], by, "tp")
        for s in steps[2:]:
            moving = shifted(joined(moving, s, half), by, "tp")
        came[i] = moving
    came, key_wgrad, value_wgrad = lax.optimization_barrier((came, key_wgrad, value_wgrad))
    hidden_grad = jnp.concatenate([
        part[0, h].astype(F32) + came[h].astype(F32) + came[3 - h].astype(F32)
        for h in range(2)
    ]).astype(BF16)
    return (
        att[None],
        dq[None],
        hidden_grad[None],
        key_wgrad,
        value_wgrad,
    )


def solution(mesh):
    fine = Mesh(
        mesh.devices.reshape(mesh.shape["dp"], mesh.shape["ctx"] // 2, 2, mesh.shape["tp"]),
        ("dp", "y", "core", "tp"),
    )
    ctx = ("y", "core")
    in_specs = (
        P("dp", ("y", "core", "tp"), None),
        P(None, "tp"),
        P(None, "tp"),
        P("dp", ctx, "tp"),
        P("dp", ctx, "tp"),
        P("dp", ctx),
    )
    out_specs = (
        P("dp", ctx, "tp"),
        P("dp", ctx, "tp"),
        P("dp", ("y", "core", "tp"), None),
        P(("dp", "y", "core"), "tp"),
        P(("dp", "y", "core"), "tp"),
    )
    return jax.shard_map(
        on_device, mesh=fine, in_specs=in_specs, out_specs=out_specs, check_vma=False
    )
```

```python
import functools
import math

import jax
import jax.numpy as jnp
from jax import lax
from jax.experimental import pallas as pl
from jax.experimental.pallas import tpu as pltpu
from jax.sharding import Mesh, PartitionSpec as P

HD = 128
SLOTS = 5
PAIR = 4
EARLY = [(s, h) for s in (0, 1, 7, 2, 6) for h in (0, 1)] + [(3, 0), (5, 1)]
LATE = [(3, 1), (5, 0), (4, 0), (4, 1)]
FIRST = [(4, 0), (3, 1), (4, 1), (5, 0), (3, 0), (2, 1), (5, 1), (6, 0)]
REST = [(s, h) for s in range(8) for h in (0, 1) if (s, h) not in FIRST]
NEG = -1e30
MIB = 1024 * 1024
VMEM = 56 * MIB
F32 = jnp.float32
BF16 = jnp.bfloat16


def attention_kernel(place_ref, kv0, kv1, kv2, kv3, near, far, q_ref, do_ref,
                     att_ref, dq_ref, p0, p1, p2, p34,
                     k_all, v_all, kt_all, vt_all, s_ref, pb_ref, ds_ref, dp_ref, dkv_ref, thr_ref):
    rows = q_ref.shape[0]
    scale = 1.0 / math.sqrt(HD)
    log2e = math.log2(math.e)
    step = pl.program_id(0)
    heads = range(PAIR)
    spans = [pl.ds(j * rows, rows) for j in range(SLOTS)]

    @pl.when(step == 0)
    def _():
        blocks = (kv0[...], kv1[...], kv2[...], kv3[...], near[...] + far[...])
        documents = [kv[rows:, :].astype(F32) for kv in blocks]
        start = jnp.full((1, rows), (1 - SLOTS) * rows, jnp.int32)
        for doc in documents:
            earlier = doc.T[:, :1] < documents[0][:1, :]
            start = start + jnp.sum(earlier.astype(jnp.int32), axis=0, keepdims=True)
        core = place_ref[2]
        for j, back in enumerate((0, 2, 4, 1 + 2 * core, 3 - 2 * core)):
            thr_ref[j:j + 1, :] = start + back * rows
        for here, kv in zip(spans, blocks):
            k = kv[:rows, :HD]
            v = kv[:rows, HD:]
            k_all[here, :] = k
            v_all[here, :] = v
            kt_all[:, here] = k.T
            vt_all[:, here] = v.T
        dkv_ref[...] = jnp.zeros_like(dkv_ref)

    q = [q_ref[:, h * HD:(h + 1) * HD] for h in heads]
    do = [do_ref[:, h * HD:(h + 1) * HD] for h in heads]
    q_t = [a.T for a in q]
    do_t = [a.T for a in do]
    top = [jnp.full((1, rows), NEG, F32) for _ in heads]
    place = lax.broadcasted_iota(jnp.int32, (rows, rows), 0)
    for j, here in enumerate(spans):
        mask = place >= thr_ref[j:j + 1, :]
        if j == 0:
            mask = mask & (place <= lax.broadcasted_iota(jnp.int32, (rows, rows), 1))
        for h in heads:
            s = jnp.dot(k_all[here, :], q_t[h], preferred_element_type=F32)
            s = jnp.where(mask, s, NEG)
            s_ref[h, here, :] = s
            top[h] = jnp.maximum(top[h], jnp.max(s, axis=0, keepdims=True))
    total = [jnp.zeros((1, rows), F32) for _ in heads]
    for here in spans:
        for h in heads:
            e = jnp.exp2((s_ref[h, here, :] - top[h]) * (scale * log2e))
            s_ref[h, here, :] = e
            total[h] = total[h] + jnp.sum(e, axis=0, keepdims=True)
            dp_ref[h, here, :] = jnp.dot(v_all[here, :], do_t[h], preferred_element_type=F32)
    inv = [1.0 / t for t in total]
    for here in spans:
        for h in heads:
            pb_ref[h, here, :] = (s_ref[h, here, :] * inv[h]).astype(BF16)
    delta = []
    for h in heads:
        out_b = jnp.dot(vt_all[...], pb_ref[h], preferred_element_type=F32).astype(BF16)
        att_ref[:, h * HD:(h + 1) * HD] = out_b.T
        delta.append(jnp.sum(do_t[h].astype(F32) * out_b.astype(F32), axis=0, keepdims=True))
    for here in spans:
        dk = jnp.zeros((rows, HD), F32)
        dv = jnp.zeros((rows, HD), F32)
        for h in heads:
            ds = (s_ref[h, here, :] * inv[h] * (dp_ref[h, here, :] - delta[h])).astype(BF16)
            ds_ref[h, here, :] = ds
            dk = dk + jnp.dot(ds, q[h], preferred_element_type=F32)
            dv = dv + jnp.dot(pb_ref[h, here, :], do[h], preferred_element_type=F32)
        dkv_ref[here, :HD] += dk
        dkv_ref[here, HD:] += dv
    for h in heads:
        dq_t = jnp.dot(kt_all[...], ds_ref[h], preferred_element_type=F32)
        dq_ref[:, h * HD:(h + 1) * HD] = (dq_t * scale).astype(BF16).T

    @pl.when(step == pl.num_programs(0) - 1)
    def _():
        for here, out in zip(spans, (p0, p1, p2, p34.at[0], p34.at[1])):
            out[:, :HD] = dkv_ref[here, :HD] * scale
            out[:, HD:] = dkv_ref[here, HD:]


def attention(place, slots, q, do):
    rows, width = q.shape
    heads = width // HD
    keys = SLOTS * rows
    whole = lambda h, place: (0, 0)
    square = pl.BlockSpec((rows, 2 * HD), whole)
    pair = pl.BlockSpec((rows, PAIR * HD), lambda h, place: (0, h))
    part = jax.ShapeDtypeStruct((rows, 2 * HD), F32)
    return pl.pallas_call(
        attention_kernel,
        grid_spec=pltpu.PrefetchScalarGridSpec(
            num_scalar_prefetch=1,
            grid=(heads // PAIR,),
            in_specs=[pl.BlockSpec(slots[0].shape, whole)] * len(slots) + [pair] * 2,
            out_specs=[
                pair, pair, square, square, square,
                pl.BlockSpec((2, rows, 2 * HD), lambda h, place: (0, 0, 0)),
            ],
            scratch_shapes=[
                pltpu.VMEM((keys, HD), BF16),
                pltpu.VMEM((keys, HD), BF16),
                pltpu.VMEM((HD, keys), BF16),
                pltpu.VMEM((HD, keys), BF16),
                pltpu.VMEM((PAIR, keys, rows), F32),
                pltpu.VMEM((PAIR, keys, rows), BF16),
                pltpu.VMEM((PAIR, keys, rows), BF16),
                pltpu.VMEM((PAIR, keys, rows), F32),
                pltpu.VMEM((keys, 2 * HD), F32),
                pltpu.VMEM((8, rows), jnp.int32),
            ],
        ),
        out_shape=[
            jax.ShapeDtypeStruct((rows, width), BF16),
            jax.ShapeDtypeStruct((rows, width), BF16),
            part, part, part,
            jax.ShapeDtypeStruct((2, rows, 2 * HD), F32),
        ],
        compiler_params=pltpu.CompilerParams(vmem_limit_bytes=30 * MIB),
        cost_estimate=pl.CostEstimate(
            flops=12 * keys * width * rows, bytes_accessed=6 * MIB,
            transcendentals=keys * rows * heads,
        ),
    )(place, *slots, q, do)


def token(place, s, h, ring, few):
    return pl.multiple_of((lax.rem(place[3] + ring - s, ring) * 2 + h) * few, few)


def project_kernel(order, ring, last, place_ref, *refs):
    pieces, refs = refs[:len(order)], refs[len(order):]
    if last:
        wk_hbm, wv_hbm, seg_hbm, early_hbm, refs = *refs[:4], refs[6:]
        *refs, seg_ref, early_ref, come_rest = refs
    else:
        wk_hbm, wv_hbm, refs = *refs[:2], refs[2:]
    kv_ref, mine_hbm, theirs_hbm, h_ref, w_ref, come, come_w, go = refs
    few = pieces[0].shape[0]
    rows, width = h_ref.shape
    block = 2 * HD
    steps = come_w.shape[0] // 2
    depth = width // steps

    copies = [
        pltpu.make_async_copy(piece, h_ref.at[pl.ds(i * few, few), :], come.at[i])
        for i, piece in enumerate(pieces)
    ]
    weights = []
    for c in range(steps):
        at = pl.ds(c * depth, depth)
        weights.append([
            pltpu.make_async_copy(
                w.at[at, :], w_ref.at[i, at, :], come_w.at[2 * c + i]
            )
            for i, w in enumerate((wk_hbm, wv_hbm))
        ])
    rest = []
    if last:
        rest = [
            pltpu.make_async_copy(seg_hbm, seg_ref, come_rest.at[0]),
            pltpu.make_async_copy(early_hbm, early_ref, come_rest.at[1]),
        ]
    for copy in weights[0] + copies + sum(weights[1:], []) + rest:
        copy.start()
    for copy in copies:
        copy.wait()
    out = []
    base = 0 if not last else len(EARLY) * few
    for i in range(width // block):
        core, to = ((1 - place_ref[2], theirs_hbm), (place_ref[2], mine_hbm))[i % 2]
        first = pl.multiple_of((2 * (i // 2) + core) * block, block)
        out.append(pltpu.make_async_copy(
            h_ref.at[:, pl.ds(first, block)],
            to.at[pl.ds(base, rows), pl.ds(i // 2 * block, block)],
            go.at[i],
        ))
        out[-1].start()
    kv = jnp.zeros((rows, 2 * HD), F32)
    for c in range(steps):
        for copy in weights[c]:
            copy.wait()
        at = slice(c * depth, (c + 1) * depth)
        h = h_ref[:, at]
        kv = kv + jnp.concatenate(
            [jnp.dot(h, w_ref[i, at, :], preferred_element_type=F32) for i in range(2)], axis=1
        )
    kv = kv.astype(BF16)
    for copy in rest:
        copy.wait()
    if not last:
        kv_ref[...] = kv
    else:
        for i, (s, h) in enumerate(order):
            kv_ref[pl.ds(token(place_ref, s, h, ring, few), few), :] = kv[i * few:(i + 1) * few]
        for i, (s, h) in enumerate(EARLY):
            to = pl.ds(token(place_ref, s, h, ring, few), few)
            kv_ref[to, :] = early_ref[i * few:(i + 1) * few, :]
        total = seg_ref.shape[1]
        own = (seg_ref[...] + 1).astype(F32)
        kv_ref[total:, :] = jnp.broadcast_to(own, (kv_ref.shape[0] - total, total)).astype(BF16)
    for copy in out:
        copy.wait()


def project(place, order, pieces, key_weight, value_weight, ring, rest=()):
    few, width = pieces[0].shape
    rows = few * len(pieces)
    total = few * 2 * ring
    steps = 4
    far = pl.BlockSpec(memory_space=pl.ANY)
    whole = lambda i, place: (0, 0)
    kv_rows = total + 16 if rest else rows
    n = len(pieces)
    return pl.pallas_call(
        functools.partial(project_kernel, order, ring, bool(rest)),
        grid_spec=pltpu.PrefetchScalarGridSpec(
            num_scalar_prefetch=1,
            grid=(1,),
            in_specs=[far] * (n + 2)
            + [far] * len(rest),
            out_specs=[pl.BlockSpec((kv_rows, 2 * HD), whole), far, far],
            scratch_shapes=[
                pltpu.VMEM((rows, width), BF16),
                pltpu.VMEM((2, width, HD), BF16),
                pltpu.SemaphoreType.DMA((n,)),
                pltpu.SemaphoreType.DMA((2 * steps,)),
                pltpu.SemaphoreType.DMA((width // (2 * HD),)),
            ]
            + ([pltpu.VMEM(a.shape, a.dtype) for a in rest[:2]] if rest else [])
            + ([pltpu.SemaphoreType.DMA((2,))] if rest else []),
        ),
        out_shape=[
            jax.ShapeDtypeStruct((kv_rows, 2 * HD), BF16),
            jax.ShapeDtypeStruct((total, width // 2), BF16),
            jax.ShapeDtypeStruct((total, width // 2), BF16),
        ],
        input_output_aliases={n + 5: 1, n + 6: 2} if rest else {},
        compiler_params=pltpu.CompilerParams(vmem_limit_bytes=VMEM),
        cost_estimate=pl.CostEstimate(
            flops=4 * rows * width * HD, bytes_accessed=8 * MIB, transcendentals=0
        ),
    )(place, *pieces, key_weight, value_weight, *rest)


def weight_grad_kernel(ring, place_ref, g_ref, gs_ref, *refs):
    hidden, (out_ref, grads_t, turn) = refs[:8], refs[8:]
    few = g_ref.shape[0] // (2 * ring)

    @pl.when(pl.program_id(0) == 0)
    def _():
        for p, g in enumerate((g_ref, gs_ref)):
            for i, (s, h) in enumerate(EARLY + LATE):
                turn[i * few:(i + 1) * few, :] = g[pl.ds(token(place_ref, s, h, ring, few), few), :]
            grads_t[p] = turn[...].T

    for i, (mine, other) in enumerate(zip(hidden[:4], hidden[4:])):
        out_ref[i] = (
            jnp.dot(grads_t[0], mine[...], preferred_element_type=F32)
            + jnp.dot(grads_t[1], other[...], preferred_element_type=F32)
        ).astype(BF16)


def weight_grad(place, grads, other_grads, mine, other, nx, ny, ring):
    rows, cols = grads.shape
    block = mine.shape[1] // (nx * ny)
    flat = pl.BlockSpec((rows, cols), lambda r, place: (0, 0))

    def column(i):
        return pl.BlockSpec((rows, block), lambda r, place: (0, r * ny + i))

    return pl.pallas_call(
        functools.partial(weight_grad_kernel, ring),
        grid_spec=pltpu.PrefetchScalarGridSpec(
            num_scalar_prefetch=1,
            grid=(nx,),
            in_specs=[flat, flat] + [column(i) for i in range(ny)] * 2,
            out_specs=pl.BlockSpec((ny, cols, block), lambda r, place: (r, 0, 0)),
            scratch_shapes=[pltpu.VMEM((2, cols, rows), BF16), pltpu.VMEM((rows, cols), BF16)],
        ),
        out_shape=jax.ShapeDtypeStruct((nx * ny, cols, block), BF16),
        compiler_params=pltpu.CompilerParams(vmem_limit_bytes=10 * MIB),
        cost_estimate=pl.CostEstimate(
            flops=4 * rows * cols * block * nx * ny, bytes_accessed=6 * MIB, transcendentals=0
        ),
    )(place, grads, other_grads, *[mine] * ny, *[other] * ny)


def finish_kernel(parts, key_ref, value_ref):
    total = parts[0].astype(F32)
    for i in range(1, parts.shape[0]):
        total = total + parts[i].astype(F32)
    key_ref[...] = total[:HD].T
    value_ref[...] = total[HD:].T


def finish(parts):
    _, cols, block = parts.shape
    n = parts.shape[0]
    half = pl.BlockSpec((block // 2, HD), lambda i: (i, 0))
    shape = jax.ShapeDtypeStruct((block, HD), F32)
    return pl.pallas_call(
        finish_kernel,
        grid=(2,),
        in_specs=[pl.BlockSpec((n, cols, block // 2), lambda i: (0, 0, i))],
        out_specs=[half, half],
        out_shape=[shape, shape],
        compiler_params=pltpu.CompilerParams(vmem_limit_bytes=8 * MIB),
    )(parts)


def spread_kernel(order, ring, place_ref, g_ref, wk_ref, wv_ref, *refs):
    outs, rows = refs[:-1], refs[-1]
    few = outs[0].shape[0]

    @pl.when(pl.program_id(0) == 0)
    def _():
        for i, (s, h) in enumerate(order):
            rows[i * few:(i + 1) * few, :] = g_ref[
                pl.ds(token(place_ref, ring - s, h, ring, few), few), :
            ]

    contract = (((1,), (1,)), ((), ()))
    part = lax.dot_general(
        rows[:, :HD], wk_ref[...], contract, preferred_element_type=F32
    ) + lax.dot_general(rows[:, HD:], wv_ref[...], contract, preferred_element_type=F32)
    for i, out in enumerate(outs):
        out[...] = part[i * few:(i + 1) * few].astype(BF16)


def spread(place, order, grads, key_weight, value_weight, ring):
    rows, cols = grads.shape
    few = rows // (2 * ring)
    width = key_weight.shape[0]
    tile = width // 8
    weight = pl.BlockSpec((tile, HD), lambda i, place: (i, 0))
    return pl.pallas_call(
        functools.partial(spread_kernel, order, ring),
        grid_spec=pltpu.PrefetchScalarGridSpec(
            num_scalar_prefetch=1,
            grid=(width // tile,),
            in_specs=[pl.BlockSpec((rows, cols), lambda i, place: (0, 0)), weight, weight],
            out_specs=[pl.BlockSpec((few, tile), lambda i, place: (0, i))] * len(order),
            scratch_shapes=[pltpu.VMEM((few * len(order), cols), BF16)],
        ),
        out_shape=[jax.ShapeDtypeStruct((few, width), BF16)] * len(order),
        compiler_params=pltpu.CompilerParams(vmem_limit_bytes=8 * MIB),
        cost_estimate=pl.CostEstimate(
            flops=2 * few * len(order) * cols * width, bytes_accessed=6 * MIB, transcendentals=0
        ),
    )(place, grads, key_weight, value_weight)


def on_device(hidden, key_weight, value_weight, queries, out_grad, segment_ids):
    rows = queries.shape[1]
    x_count, width = hidden.shape[1:]
    nx = lax.axis_size("dp")
    ny = lax.axis_size("y")
    heads = lax.axis_size("tp")
    x = lax.axis_index("dp")
    core = lax.axis_index("core")
    place = jnp.stack([x, lax.axis_index("y"), core, lax.axis_index("tp")]).astype(jnp.int32)
    swap = [(0, 1), (1, 0)]

    def swapped(a):
        return lax.ppermute(a, "core", swap)

    def shifted(a, s, axis="dp"):
        n = lax.axis_size(axis)
        return lax.ppermute(a, axis, [(i, (i + s) % n) for i in range(n)])

    half = x_count // 2
    ring = {(0, h): hidden[0, h * half:(h + 1) * half] for h in range(2)}
    for s in range(1, heads // 2 + 1):
        for h in range(2):
            if s < heads // 2 or h == 0:
                ring[s, h] = shifted(ring[s - 1, h], 1, "tp")
            if s < heads // 2 or h == 1:
                ring[heads - s, h] = shifted(ring[(heads - s + 1) % heads, h], -1, "tp")
    weights = (key_weight, value_weight)
    early = project(place, EARLY, [ring[i] for i in EARLY], *weights, heads)
    kv, mine, theirs = project(
        place, LATE, [ring[i] for i in LATE], *weights, heads, (segment_ids, *early)
    )

    down1 = [(i, i + 1) for i in range(ny - 1)]
    down2 = [(i, i + 2) for i in range(ny - 2)]
    kv1 = lax.ppermute(kv, "y", down1)
    kv2 = lax.ppermute(kv, "y", down2)
    near = lax.ppermute(kv, "core", [(0, 1)])
    kv3 = swapped(kv1)
    far = lax.ppermute(kv2, "core", [(1, 0)])

    att, dq, part0, part1, part2, part34 = attention(
        place, (kv, kv1, kv2, kv3, near, far), queries[0], out_grad[0]
    )

    up1 = [(i + 1, i) for i in range(ny - 1)]
    up2 = [(i + 2, i) for i in range(ny - 2)]
    got = swapped(part34)
    send1 = (part1 + got[0]).astype(BF16)
    send2 = (part2 + jnp.where(core == 0, 0.0, got[1])).astype(BF16)
    own = part0 + jnp.where(core == 0, got[1], 0.0)
    got1 = lax.ppermute(send1, "y", up1)
    got2 = lax.ppermute(send2, "y", up2)
    grads = (own + got1.astype(F32) + got2.astype(F32)).astype(BF16)

    other_grads = swapped(grads)
    part = dict(zip(FIRST, spread(place, FIRST, grads, *weights, heads)))
    other = swapped(theirs)
    grads, _ = lax.optimization_barrier((grads, part))
    sums = weight_grad(place, grads, other_grads, mine, other, nx, ny, heads)
    grads, sums = lax.optimization_barrier((grads, sums))
    part.update(zip(REST, spread(place, REST, grads, *weights, heads)))

    def joined(moving, s, half):
        return (moving.astype(F32) + part[s, half].astype(F32)).astype(BF16)

    routes = [
        (0, (4, 3, 2, 1), 1), (1, (4, 5, 6, 7), -1), (1, (3, 2, 1), 1), (0, (5, 6, 7), -1)
    ]
    came = [shifted(part[steps[0], half], by, "tp") for half, steps, by in routes]
    sums, *came[:2] = lax.optimization_barrier((sums, *came[:2]))
    came[:2] = [joined(moving, steps[1], half) for moving, (half, steps, _) in zip(came, routes[:2])]
    sums, *came[:2] = lax.optimization_barrier((sums, *came[:2]))
    _, *came[2:] = lax.optimization_barrier((came[0], *came[2:]))
    came[2:] = [joined(moving, steps[1], half) for moving, (half, steps, _) in zip(came[2:], routes[2:])]
    key_wgrad, value_wgrad = finish(lax.all_to_all(sums, ("dp", "y"), 0, 0, tiled=True))
    for i, (half, steps, by) in enumerate(routes):
        moving = shifted(came[i], by, "tp")
        for s in steps[2:]:
            moving = shifted(joined(moving, s, half), by, "tp")
        came[i] = moving
    came, key_wgrad, value_wgrad = lax.optimization_barrier((came, key_wgrad, value_wgrad))
    hidden_grad = jnp.concatenate([
        part[0, h].astype(F32) + came[h].astype(F32) + came[3 - h].astype(F32)
        for h in range(2)
    ]).astype(BF16)
    return (
        att[None],
        dq[None],
        hidden_grad[None],
        key_wgrad,
        value_wgrad,
    )


def solution(mesh):
    fine = Mesh(
        mesh.devices.reshape(mesh.shape["dp"], mesh.shape["ctx"] // 2, 2, mesh.shape["tp"]),
        ("dp", "y", "core", "tp"),
    )
    ctx = ("y", "core")
    in_specs = (
        P("dp", ("y", "core", "tp"), None),
        P(None, "tp"),
        P(None, "tp"),
        P("dp", ctx, "tp"),
        P("dp", ctx, "tp"),
        P("dp", ctx),
    )
    out_specs = (
        P("dp", ctx, "tp"),
        P("dp", ctx, "tp"),
        P("dp", ("y", "core", "tp"), None),
        P(("dp", "y", "core"), "tp"),
        P(("dp", "y", "core"), "tp"),
    )
    return jax.shard_map(
        on_device, mesh=fine, in_specs=in_specs, out_specs=out_specs, check_vma=False
    )
```
